256 devices in a mesh: dp: 16 (over z, y_hi), mp: 16 (over x, y_lo, core).
Axes of the slice: x: 4, y: 4 (y_hi: 2, y_lo: 2; y = y_hi * 2 + y_lo), z: 8, core: 2. Of those that a mesh axis runs over, the one named last changes fastest.
Arguments:
- image_features: bfloat16 [1152, 18432], P('mp', 'dp'), may hold values from -6 to 6
- proj_weight: bfloat16 [1152, 1152], P('mp'), may hold values from -0.1875 to 0.1875
- text_embed: bfloat16 [18432, 1152], P(('dp', 'mp')), may hold values from -6 to 6
- text_match: int32 [18432], P(('dp', 'mp')), may hold values from 0 to 18431, as said below
- logit_scale: float32 [1], replicated, may hold values from 4 to 16
- logit_bias: float32 [1], replicated, may hold values from -2.5 to -0.5
Outputs:
- text_grad: bfloat16 [18432, 1152], P(('dp', 'mp'))
- feature_grad: bfloat16 [1152, 18432], P('mp', 'dp')
- proj_grad: float32 [1152, 1152], P('mp')
The draws below stay inside these ranges and needn't reach their ends.
Inputs may be any that keep to these rules, and one draw needn't show every extreme that they name: text_match[j] is j, or for odd j an even index below j (text j repeats the caption of that image); every even index and the last index map to themselves.
All inputs are finite; a program needn't handle non-finite values.
Results may differ from the reference program's by a relative error of at most 0.02.
Values may be sent and summed in bfloat16 or wider, within the bound.
A program may use at most 64 MiB of HBM per device.

```python
import math
import jax
import jax.numpy as jnp
from jax import lax

WIDTH = 1152
EMBED = 1152
GROUP = 1152
BATCH = 18432


def draw_text_match(key, part):
    key = jax.random.fold_in(key, 7)
    pick_key, earlier_key = jax.random.split(key)
    position = jnp.arange(BATCH, dtype=jnp.int32)
    chosen = jax.random.randint(pick_key, (BATCH,), 0, 4)
    earlier = 2 * jax.random.randint(earlier_key, (BATCH,), 0, jnp.maximum((position + 1) // 2, 1))
    repeated = (position % 2 == 1) & (chosen == 0) & (position < BATCH - 1)
    return jnp.where(repeated, earlier, position).astype(jnp.int32)


def with_spikes(drawn, rng, source, target, shards_of, factor):
    def block_of(dim):
        return (jnp.arange(drawn.shape[dim]) // (drawn.shape[dim] // shards_of)).reshape((-1,) + (1,) * (drawn.ndim - 1 - dim))

    first = jax.random.permutation(rng, shards_of)[block_of(target)]
    far = (block_of(target) + shards_of // 2) % shards_of
    return jnp.where((block_of(source) == first) | (block_of(source) == far), factor * drawn, drawn)


def levels(rng, dims, cuts, least, largest):
    factor_of, own = 1.0, jax.random.fold_in(rng, 6)
    for axis_at, blocks in cuts:
        steps = jnp.exp(jax.random.uniform(jax.random.fold_in(own, axis_at), (blocks,), jnp.float32, least / len(cuts), largest / len(cuts)))
        factor_of = factor_of * jnp.repeat(steps, dims[axis_at] // blocks).reshape([-1 if axis == axis_at else 1 for axis in range(len(dims))])
    return factor_of


def normal_values(stream_key, shape, deviation, bound, shards=(), held_as=jnp.bfloat16):
    result = deviation * jax.random.normal(stream_key, shape, jnp.float32)
    if shards:
        result = result * levels(stream_key, shape, shards, -0.22, 0.18)
    return jnp.clip(result, -bound, bound).astype(held_as)


def heavy_noise(own_key, shape, scale, reach, cuts, heavy, kind=jnp.bfloat16):
    values = scale * jax.random.normal(own_key, shape, jnp.float32)
    if cuts:
        values = values * levels(own_key, shape, cuts, -0.22, 0.18)
    return jnp.clip(with_spikes(values, jax.random.fold_in(own_key, 3), *heavy), -reach, reach).astype(kind)


def setup_inputs(seed: int = 0) -> dict:
    key_of = jax.random.split(jax.random.key(seed), 7)
    image_features = heavy_noise(key_of[0], (WIDTH, BATCH), 1.0, 6.0, ((0, 16), (1, 16)), (0, 1, 16, 2.0))
    proj_weight = normal_values(key_of[1], (WIDTH, EMBED), WIDTH ** -0.5, 0.1875, ((0, 16),))
    text_embed = normal_values(key_of[2], (BATCH, EMBED), 1.0, 6.0, ((0, 256),))
    text_match = draw_text_match(jax.random.fold_in(key_of[6], 71), 0)
    logit_scale = jnp.clip(jnp.exp(jax.random.uniform(key_of[4], (1,), jnp.float32, math.log(4.0), math.log(16.0))), 4.0, 16.0)
    logit_bias = jnp.clip(jax.random.uniform(key_of[5], (1,), jnp.float32, -2.5, -0.5), -2.5, -0.5)
    return dict(image_features=image_features, proj_weight=proj_weight, text_embed=text_embed, text_match=text_match, logit_scale=logit_scale, logit_bias=logit_bias)


norm_floor = 1e-06

def inverse_norm(values):
    return lax.rsqrt(lax.optimization_barrier(jnp.sum(values * values, axis=1, keepdims=True)) + norm_floor)

def norm_backward(values, inverse, upstream):
    along = lax.optimization_barrier(jnp.sum(values * upstream, axis=1, keepdims=True))
    return inverse * upstream - inverse * inverse * inverse * along * values

def pair_tile(image_unit, image_index, text_unit, text_match, text_index, scaling, offset):
    products = lax.dot_general(text_unit, image_unit, (((1,), (1,)), ((), ())), preferred_element_type=jnp.float32)
    logits = scaling * products + offset
    positive = (text_index[:, None] == image_index[None, :]) | (text_match[:, None] == image_index[None, :])
    signs = jnp.where(positive, 1.0, -1.0).astype(jnp.float32)
    pair_coef = (-signs * scaling * jax.nn.sigmoid(-signs * logits)).astype(jnp.bfloat16)
    text_part = jnp.dot(pair_coef, image_unit, preferred_element_type=jnp.float32)
    image_part = lax.dot_general(pair_coef, text_unit, (((0,), (0,)), ((), ())), preferred_element_type=jnp.float32)
    return (image_part, text_part)

def reference(image_features, proj_weight, text_embed, text_match, logit_scale, logit_bias):
    scaling = logit_scale[0]
    offset = logit_bias[0]
    projected = lax.dot_general(image_features, proj_weight, (((0,), (0,)), ((), ())), preferred_element_type=jnp.float32)
    image_inverse = inverse_norm(projected)
    image_unit = (projected * image_inverse).astype(jnp.bfloat16)
    text_values = text_embed.astype(jnp.float32)
    text_inverse = inverse_norm(text_values)
    text_unit = (text_values * text_inverse).astype(jnp.bfloat16)
    image_index = jnp.arange(BATCH, dtype=jnp.int32)
    block_count = BATCH // GROUP
    unit_blocks = text_unit.reshape(block_count, GROUP, EMBED)
    match_blocks = text_match.reshape(block_count, GROUP)
    index_blocks = image_index.reshape(block_count, GROUP)

    def visit(image_acc, text_block):
        block_unit, block_match, block_index = text_block
        image_part, text_part = pair_tile(image_unit, image_index, block_unit, block_match, block_index, scaling, offset)
        return (image_acc + image_part, text_part)
    image_acc, text_parts = lax.scan(visit, jnp.zeros((BATCH, EMBED), jnp.float32), (unit_blocks, match_blocks, index_blocks))
    text_grad_unit = text_parts.reshape(BATCH, EMBED)
    grad_projected = norm_backward(projected, image_inverse, image_acc).astype(jnp.bfloat16)
    feature_grad = lax.dot_general(proj_weight, grad_projected, (((1,), (1,)), ((), ())), preferred_element_type=jnp.float32).astype(jnp.bfloat16)
    proj_grad = jnp.dot(image_features, grad_projected, preferred_element_type=jnp.float32)
    text_grad = norm_backward(text_values, text_inverse, text_grad_unit).astype(jnp.bfloat16)
    return (text_grad, feature_grad, proj_grad)
```

```python
import functools

import jax
import jax.numpy as jnp
from jax import lax
from jax.experimental import pallas as pl
from jax.experimental.pallas import tpu as pltpu
from jax.sharding import PartitionSpec as P

MESH = pl.DeviceIdType.MESH
norm_floor = 1e-06
f32, bf16 = jnp.float32, jnp.bfloat16

ZS, XS = 8, 4
ROWS = 72
PAD = 80
BLOCK = 144
HEAD = 80
GROUP = 1152
EMBED = 1152
CHUNK = 288
TILE = 384
TEXT_ORDER = (4, -3, 3, -2, 2, -1, 1, 0)
TEXT_POS = {step: at for at, step in enumerate(TEXT_ORDER)}
IMAGE_ORDER = (2, 1, 3, 0)
PIECES, PIECE_ROWS, PIECE_COLS = 15, 16, 384
SEMS = 160


def inverse_norm(values):
    return lax.rsqrt(jnp.sum(values * values, axis=1, keepdims=True) + norm_floor)


def norm_backward(values, inverse, upstream):
    along = jnp.sum(values * upstream, axis=1, keepdims=True)
    return inverse * upstream - inverse * inverse * inverse * along * values


def kernel(
    scale_ref, bias_ref, f_ref, w_ref, t_ref, m_ref,
    tg_ref, fg_ref, pg_ref,
    xsend, xrecv, fw, tsend, trecv, msend, mrecv, tn, mt, mcol, proj, unit, logits, coef, dt, du,
    tout, tra, tlb, tr, tl, ysend_t, yrecv_t,
    csend, crecv, xout, xra, xlb, xr, xl, yout, yin, gp,
    ws, wr, wa,
    send_sem, recv_sem,
):
    d, m = lax.axis_index("dp"), lax.axis_index("mp")
    z, yhi = d // 2, d % 2
    x, ylo, core = m // 4, (m // 2) % 2, m % 2

    def at_z(step):
        return {"dp": lax.rem(z + step + ZS, ZS) * 2 + yhi, "mp": m}

    def at_x(step):
        return {"dp": d, "mp": lax.rem(x + step + XS, XS) * 4 + ylo * 2 + core}

    other_yhi = {"dp": z * 2 + (1 - yhi), "mp": m}
    other_ylo = {"dp": d, "mp": x * 4 + (1 - ylo) * 2 + core}
    sibling = {"dp": d, "mp": x * 4 + ylo * 2 + (1 - core)}

    def dp_at(index):
        return {"dp": index, "mp": m}

    barrier = pltpu.get_barrier_semaphore()
    partners = [sibling, other_ylo, at_x(1), at_x(-1)]
    partners += [dp_at(lax.rem(d + step, 16)) for step in range(1, 16)]
    for partner in partners:
        pl.semaphore_signal(barrier, inc=1, device_id=partner, device_id_type=MESH)

    keys = {}

    def key(name):
        return keys.setdefault(name, len(keys))

    def describe(name, src, dst, target):
        k = key(name)
        return pltpu.make_async_remote_copy(
            src_ref=src, dst_ref=dst, send_sem=send_sem.at[k], recv_sem=recv_sem.at[k],
            device_id=target, device_id_type=MESH,
        )

    sent = []

    def start(name, src, dst, target):
        copy = describe(name, src, dst, target)
        copy.start()
        sent.append(copy)

    def arrived(name, dst, target=sibling):
        describe(name, dst, dst, target).wait_recv()

    f_mine, w_mine = f_ref[...].astype(f32), w_ref[...].astype(f32)
    is_first = core == 0
    pad_rows = jnp.zeros((PAD - ROWS, EMBED), f32)
    xsend[...] = jnp.concatenate([jnp.where(is_first, w_mine, f_mine), pad_rows]).astype(bf16)
    text_values = t_ref[...].astype(f32)
    text_inverse = inverse_norm(text_values)
    text_mine = text_values * text_inverse
    tsend[...] = jnp.concatenate([text_mine, pad_rows]).astype(bf16)
    msend[...] = jnp.zeros_like(msend)
    msend[0:1, 0:ROWS] = m_ref[...]
    pl.semaphore_wait(barrier, len(partners))

    start("x0", xsend, xrecv, sibling)
    start("t0", tsend, trecv, other_yhi)
    start("m0", msend, mrecv, other_yhi)

    def slot(index, count=1):
        return pl.ds(index * BLOCK, count * BLOCK)

    def mine(index):
        return fw.at[core, slot(index)]

    def share(index):
        start(("fs", index), mine(index), mine(index), sibling)

    arrived("x0", xrecv)
    own = jnp.where(is_first, f_mine, w_mine)
    theirs = xrecv[...].astype(f32)[:ROWS]
    fw[core, slot(0), :] = jnp.concatenate(
        [jnp.where(is_first, own, theirs), jnp.where(is_first, theirs, own)]
    ).astype(bf16)
    start(("fx", 4), mine(0), mine(4), at_x(1))
    start(("fx", 2), mine(0), mine(2), at_x(-1))
    start(("fx", 1), mine(0), mine(1), other_ylo)
    share(0)

    def text_at(step):
        return pl.ds(TEXT_POS[step] * BLOCK, BLOCK)

    def text_forward(step, target, new_step):
        start(("t", new_step), tn.at[text_at(step)], tn.at[text_at(new_step)], target)
        start(("m", new_step), mt.at[TEXT_POS[step]], mt.at[TEXT_POS[new_step]], target)

    def text_arrived(step):
        arrived(("t", step), tn.at[text_at(step)])
        arrived(("m", step), mt.at[TEXT_POS[step]])

    is_low = yhi == 0
    arrived("t0", trecv)
    arrived("m0", mrecv)
    theirs = trecv[...].astype(f32)[:ROWS]
    text_mine = tsend[...].astype(f32)[:ROWS]
    tn[text_at(0), :] = jnp.concatenate(
        [jnp.where(is_low, text_mine, theirs), jnp.where(is_low, theirs, text_mine)]
    ).astype(bf16)
    match_mine, match_theirs = msend[0:1, :], mrecv[0:1, :]
    mt[TEXT_POS[0], 0:1, :] = jnp.where(is_low, match_mine, match_theirs)
    mt[TEXT_POS[0], 1:2, :] = jnp.where(is_low, match_theirs, match_mine)
    mt[TEXT_POS[0], 2:8, :] = jnp.zeros((6, 128), jnp.int32)
    text_forward(0, at_z(1), -1)
    text_forward(0, at_z(-1), 1)

    arrived(("fx", 1), mine(1))
    start(("fx", 5), mine(1), mine(5), at_x(1))
    start(("fx", 3), mine(1), mine(3), at_x(-1))
    share(1)
    arrived(("fx", 4), mine(4))
    start(("fx", 6), mine(4), mine(6), at_x(1))
    share(4)
    arrived(("fx", 2), mine(2))
    share(2)
    text_arrived(-1)
    text_forward(-1, at_z(1), -2)
    text_arrived(1)
    text_forward(1, at_z(-1), 2)
    arrived(("fx", 3), mine(3))
    start(("fx", 7), mine(3), mine(7), at_x(-1))
    share(3)
    arrived(("fx", 5), mine(5))
    share(5)
    text_arrived(-2)
    text_forward(-2, at_z(1), -3)
    text_arrived(2)
    text_forward(2, at_z(-1), 3)
    arrived(("fx", 6), mine(6))
    share(6)
    arrived(("fx", 7), mine(7))
    share(7)

    def far_text(step, start_row, rows, target):
        src = tn.at[pl.ds(TEXT_POS[step] * BLOCK + start_row, rows)]
        dst = tn.at[pl.ds(TEXT_POS[4] * BLOCK + start_row, rows)]
        return src, dst

    text_arrived(-3)
    src, dst_head = far_text(-3, 0, HEAD, None)
    start(("t", 4, 0), src, dst_head, at_z(1))
    start(("m", 4), mt.at[TEXT_POS[-3]], mt.at[TEXT_POS[4]], at_z(1))
    text_arrived(3)
    src, dst_tail = far_text(3, HEAD, BLOCK - HEAD, None)
    start(("t", 4, 1), src, dst_tail, at_z(-1))

    for index in range(8):
        arrived(("fs", index), fw.at[1 - core, slot(index)])

    def project(tile, _):
        columns = pl.ds(pl.multiple_of(tile * TILE, TILE), TILE)
        values = lax.dot_general(
            fw[0, :, columns], fw[1], (((0,), (0,)), ((), ())), preferred_element_type=f32
        )
        normal = (values * inverse_norm(values)).astype(bf16)
        for part in range(TILE // 96):
            piece = tile * (TILE // 96) + part
            away = lax.rem(piece // 3 - x + XS, XS)
            place = jnp.where(away == 2, 0, jnp.where(away == 1, 1, jnp.where(away == 3, 2, 3)))
            row = pl.multiple_of(place * CHUNK + (piece % 3) * 96, 96)
            proj[pl.ds(row, 96), :] = values[part * 96:(part + 1) * 96]
            unit[pl.ds(row, 96), :] = normal[part * 96:(part + 1) * 96]
        return 0

    lax.fori_loop(0, GROUP // TILE, project, 0)

    lane = lax.broadcasted_iota(jnp.int32, (1, GROUP), 1)
    image_index = jnp.zeros_like(lane)
    for place, away in enumerate(IMAGE_ORDER):
        base = d * GROUP + lax.rem(x + away, XS) * CHUNK - place * CHUNK
        image_index = jnp.where(lane // CHUNK == place, base + lane, image_index)

    arrived(("t", 4, 0), dst_head)
    arrived(("t", 4, 1), dst_tail)
    arrived(("m", 4), mt.at[TEXT_POS[4]])

    row_number = lax.broadcasted_iota(jnp.int32, (ROWS, 128), 0)
    for place, step in enumerate(TEXT_ORDER):
        from_z = lax.rem(z + step + ZS, ZS)
        for high in range(2):
            row = mt[place, high:high + 1, :]
            column = jnp.transpose(jnp.broadcast_to(row, (128, 128)))[:ROWS]
            rows = pl.ds(place * BLOCK + high * ROWS, ROWS)
            mcol[0, rows, :] = column
            mcol[1, rows, :] = ((from_z * 2 + high) * 16 + m) * ROWS + row_number

    scaling, offset = scale_ref[0], bias_ref[0]

    def pairs(chunk):
        rows = pl.ds(chunk * CHUNK, CHUNK)
        logits[...] = lax.dot_general(
            tn[rows, :], unit[...], (((1,), (1,)), ((), ())), preferred_element_type=f32
        )

        def coefficients(step, _):
            at = pl.multiple_of(step * 16, 16)
            here = pl.ds(chunk * CHUNK + at, 16)
            match = mcol[0, here, 0:1]
            index = mcol[1, here, 0:1]
            positive = (index == image_index) | (match == image_index)
            factor = jnp.where(positive, -scaling, scaling)
            shift = jnp.where(positive, -offset, offset)
            values = factor * logits[pl.ds(at, 16), :] + shift
            coef[here, :] = (factor / (1.0 + jnp.exp(-values))).astype(bf16)
            return 0

        lax.fori_loop(0, CHUNK // 16, coefficients, 0)
        dt[rows, :] = jnp.dot(coef[rows, :], unit[...], preferred_element_type=f32)

    def text_partial(step):
        return dt[text_at(step), :]

    def text_out(step, values, name, dst, target):
        place = TEXT_POS[step]
        tout[place] = values.astype(bf16)
        start(name, tout.at[place], dst, target)

    pairs(0)
    tout[0] = text_partial(4).astype(bf16)
    start("tra", tout.at[0, pl.ds(0, HEAD)], tra, at_z(1))
    start("tlb", tout.at[0, pl.ds(HEAD, BLOCK - HEAD)], tlb, at_z(-1))
    pairs(1)
    arrived("tlb", tlb)
    values = text_partial(-3)
    values = jnp.concatenate([values[:HEAD], values[HEAD:] + tlb[...].astype(f32)])
    text_out(-3, values, ("tl", 0), tl.at[0], at_z(-1))
    arrived("tra", tra)
    values = text_partial(3)
    values = jnp.concatenate([values[:HEAD] + tra[...].astype(f32), values[HEAD:]])
    text_out(3, values, ("tr", 0), tr.at[0], at_z(1))
    pairs(2)
    pairs(3)

    def image_tile(tile):
        columns = pl.ds(tile * TILE, TILE)
        du[columns, :] = lax.dot_general(
            coef[:, columns], tn[...], (((0,), (0,)), ((), ())), preferred_element_type=f32
        )

    def image_block(place, which):
        return pl.ds(pl.multiple_of(place * CHUNK + which * BLOCK, BLOCK), BLOCK)

    def to_sibling(place):
        csend[place] = du[image_block(place, 1 - core), :].astype(bf16)
        start(("c", place), csend.at[place], crecv.at[place], sibling)

    def with_sibling(place):
        arrived(("c", place), crecv.at[place])
        return du[image_block(place, core), :] + crecv[place].astype(f32)

    def text_step(index):
        arrived(("tr", 1 - index), tr.at[1 - index])
        step = index + 1
        text_out(
            step, text_partial(step) + tr[1 - index].astype(f32), ("tr", 2 - index), tr.at[2 - index], at_z(1)
        )
        arrived(("tl", 1 - index), tl.at[1 - index])
        text_out(
            -step, text_partial(-step) + tl[1 - index].astype(f32), ("tl", 2 - index), tl.at[2 - index], at_z(-1)
        )

    image_tile(0)
    to_sibling(0)
    image_tile(1)
    to_sibling(1)
    xout[0] = with_sibling(0).astype(bf16)
    start("xra", xout.at[0, pl.ds(0, HEAD)], xra, at_x(1))
    start("xlb", xout.at[0, pl.ds(HEAD, BLOCK - HEAD)], xlb, at_x(-1))
    image_tile(2)
    to_sibling(2)
    to_sibling(3)
    text_step(1)
    values = with_sibling(1)
    arrived("xra", xra)
    xout[1] = jnp.concatenate([values[:HEAD] + xra[...].astype(f32), values[HEAD:]]).astype(bf16)
    start("xr", xout.at[1], xr, at_x(1))
    values = with_sibling(2)
    arrived("xlb", xlb)
    xout[2] = jnp.concatenate([values[:HEAD], values[HEAD:] + xlb[...].astype(f32)]).astype(bf16)
    start("xl", xout.at[2], xl, at_x(-1))
    values = with_sibling(3)
    arrived("xr", xr)
    arrived("xl", xl)
    values = values + xr[...].astype(f32) + xl[...].astype(f32)
    yout[...] = values.astype(bf16)

    def gp_block(from_x, which, start_row=0, rows=BLOCK):
        first = pl.multiple_of(from_x * CHUNK + which * BLOCK + start_row, 16)
        return gp.at[pl.ds(first, rows)]

    owner = ylo == core
    mine_gp = gp_block(x, core)
    to_owner = describe("yo", yout, yin, other_ylo)
    from_owner = describe("yg", mine_gp, mine_gp, other_ylo)

    @pl.when(jnp.logical_not(owner))
    def _():
        to_owner.start()

    text_step(0)

    @pl.when(owner)
    def _():
        to_owner.wait_recv()
        total = values + yin[...].astype(f32)
        projected = proj[image_block(3, core), :]
        first = pl.multiple_of(x * CHUNK + core * BLOCK, 16)
        gp[pl.ds(first, BLOCK), :] = norm_backward(
            projected, inverse_norm(projected), total
        ).astype(bf16)
        from_owner.start()

    @pl.when(jnp.logical_not(owner))
    def _():
        from_owner.wait_recv()

    left_x, right_x, far_x = lax.rem(x + 3, XS), lax.rem(x + 1, XS), lax.rem(x + 2, XS)
    tail_rows = BLOCK - HEAD
    start("gr", mine_gp, mine_gp, at_x(1))
    start("gl", mine_gp, mine_gp, at_x(-1))
    start("gs0", mine_gp, mine_gp, sibling)

    arrived(("tr", 2), tr.at[2])
    arrived(("tl", 2), tl.at[2])
    total = text_partial(0) + tr[2].astype(f32) + tl[2].astype(f32)
    for_other = jnp.where(is_low, total[ROWS:], total[:ROWS])
    text_total = jnp.where(is_low, total[:ROWS], total[ROWS:])
    ysend_t[...] = jnp.concatenate([for_other, pad_rows]).astype(bf16)
    start("ty", ysend_t, yrecv_t, other_yhi)

    arrived("gr", gp_block(left_x, core))
    start("gfr", gp_block(left_x, core, 0, HEAD), gp_block(left_x, core, 0, HEAD), at_x(1))
    start("gs1", gp_block(left_x, core), gp_block(left_x, core), sibling)
    arrived("gl", gp_block(right_x, core))
    start(
        "gfl", gp_block(right_x, core, HEAD, tail_rows), gp_block(right_x, core, HEAD, tail_rows), at_x(-1)
    )
    start("gs2", gp_block(right_x, core), gp_block(right_x, core), sibling)

    arrived("ty", yrecv_t)
    text_total = text_total + yrecv_t[...].astype(f32)[:ROWS]
    tg_ref[...] = norm_backward(text_values, text_inverse, text_total).astype(bf16)

    arrived("gfr", gp_block(far_x, core, 0, HEAD))
    start("gs3", gp_block(far_x, core, 0, HEAD), gp_block(far_x, core, 0, HEAD), sibling)
    arrived("gfl", gp_block(far_x, core, HEAD, tail_rows))
    start(
        "gs4", gp_block(far_x, core, HEAD, tail_rows), gp_block(far_x, core, HEAD, tail_rows), sibling
    )
    arrived("gs0", gp_block(x, 1 - core))
    arrived("gs1", gp_block(left_x, 1 - core))
    arrived("gs2", gp_block(right_x, 1 - core))
    arrived("gs3", gp_block(far_x, 1 - core, 0, HEAD))
    arrived("gs4", gp_block(far_x, 1 - core, HEAD, tail_rows))

    part = jnp.dot(f_ref[...], gp[...], preferred_element_type=f32)
    ws[...] = jnp.concatenate([part, pad_rows]).astype(bf16)

    def piece_of(index):
        rows = pl.ds(pl.multiple_of((index // 3) * PIECE_ROWS, PIECE_ROWS), PIECE_ROWS)
        columns = pl.ds(pl.multiple_of((index % 3) * PIECE_COLS, PIECE_COLS), PIECE_COLS)
        return rows, columns

    def numbered(base, to, source, src, dst, target):
        return pltpu.make_async_remote_copy(
            src_ref=src, dst_ref=dst, send_sem=send_sem.at[base + to], recv_sem=recv_sem.at[base + source],
            device_id=target, device_id_type=MESH,
        )

    base = len(keys)
    again = base + 16

    def scatter(index):
        rows, columns = piece_of(index)
        return numbered(base, index, d, ws.at[rows, columns], wr.at[d], dp_at(index))

    def gather(index):
        return numbered(again, index, d, wa.at[d], wa.at[d], dp_at(index))

    for index in range(PIECES):
        @pl.when(d != index)
        def _(index=index):
            scatter(index).start()

    fg_ref[...] = lax.dot_general(
        w_ref[...], gp[...], (((1,), (1,)), ((), ())), preferred_element_type=f32
    ).astype(bf16)

    @pl.when(d < PIECES)
    def _():
        rows, columns = piece_of(d)
        wr[d] = ws[rows, columns]
        for source in range(16):
            @pl.when(d != source)
            def _(source=source):
                numbered(base, 0, source, wr.at[source], wr.at[source], sibling).wait_recv()
        total = wr[0].astype(f32)
        for source in range(1, 16):
            total = total + wr[source].astype(f32)
        wa[d] = total.astype(bf16)
        for index in range(16):
            @pl.when(d != index)
            def _(index=index):
                gather(index).start()

    for index in range(PIECES):
        @pl.when(d != index)
        def _(index=index):
            numbered(again, 0, index, wa.at[index], wa.at[index], sibling).wait_recv()
    for index in range(PIECES):
        first = (index // 3) * PIECE_ROWS
        count = min(PIECE_ROWS, ROWS - first)
        columns = pl.ds((index % 3) * PIECE_COLS, PIECE_COLS)
        pg_ref[pl.ds(first, count), columns] = wa[index].astype(f32)[:count]

    for copy in sent:
        copy.wait_send()

    @pl.when(jnp.logical_not(owner))
    def _():
        to_owner.wait_send()

    @pl.when(owner)
    def _():
        from_owner.wait_send()

    for index in range(PIECES):
        @pl.when(d != index)
        def _(index=index):
            scatter(index).wait_send()

    @pl.when(d < PIECES)
    def _():
        for index in range(16):
            @pl.when(d != index)
            def _(index=index):
                gather(index).wait_send()


def local(image_features, proj_weight, text_embed, text_match, logit_scale, logit_bias):
    vmem = pl.BlockSpec(memory_space=pltpu.VMEM)
    smem = pl.BlockSpec(memory_space=pltpu.SMEM)
    block = (BLOCK, EMBED)
    square = (GROUP, EMBED)
    tail = BLOCK - HEAD
    scratch = [
        pltpu.VMEM((PAD, EMBED), bf16),
        pltpu.VMEM((PAD, EMBED), bf16),
        pltpu.VMEM((2,) + square, bf16),
        pltpu.VMEM((PAD, EMBED), bf16),
        pltpu.VMEM((PAD, EMBED), bf16),
        pltpu.VMEM((8, 128), jnp.int32),
        pltpu.VMEM((8, 128), jnp.int32),
        pltpu.VMEM(square, bf16),
        pltpu.VMEM((8, 8, 128), jnp.int32),
        pltpu.VMEM((2, GROUP, 128), jnp.int32),
        pltpu.VMEM(square, f32),
        pltpu.VMEM(square, bf16),
        pltpu.VMEM((CHUNK, GROUP), f32),
        pltpu.VMEM(square, bf16),
        pltpu.VMEM(square, f32),
        pltpu.VMEM(square, f32),
        pltpu.VMEM((8,) + block, bf16),
        pltpu.VMEM((HEAD, EMBED), bf16),
        pltpu.VMEM((tail, EMBED), bf16),
        pltpu.VMEM((3,) + block, bf16),
        pltpu.VMEM((3,) + block, bf16),
        pltpu.VMEM((PAD, EMBED), bf16),
        pltpu.VMEM((PAD, EMBED), bf16),
        pltpu.VMEM((4,) + block, bf16),
        pltpu.VMEM((4,) + block, bf16),
        pltpu.VMEM((3,) + block, bf16),
        pltpu.VMEM((HEAD, EMBED), bf16),
        pltpu.VMEM((tail, EMBED), bf16),
        pltpu.VMEM(block, bf16),
        pltpu.VMEM(block, bf16),
        pltpu.VMEM(block, bf16),
        pltpu.VMEM(block, bf16),
        pltpu.VMEM(square, bf16),
        pltpu.VMEM((PAD, EMBED), bf16),
        pltpu.VMEM((16, PIECE_ROWS, PIECE_COLS), bf16),
        pltpu.VMEM((16, PIECE_ROWS, PIECE_COLS), bf16),
        pltpu.SemaphoreType.DMA((SEMS,)),
        pltpu.SemaphoreType.DMA((SEMS,)),
    ]
    rows = text_embed.shape[0]
    return pl.pallas_call(
        kernel,
        out_shape=(
            jax.ShapeDtypeStruct((rows, EMBED), bf16),
            jax.ShapeDtypeStruct((rows, GROUP), bf16),
            jax.ShapeDtypeStruct((rows, EMBED), f32),
        ),
        in_specs=[smem, smem, vmem, vmem, vmem, vmem],
        out_specs=(vmem, vmem, vmem),
        scratch_shapes=scratch,
        compiler_params=pltpu.CompilerParams(
            collective_id=0, has_side_effects=True, vmem_limit_bytes=60 * 1024 * 1024
        ),
        cost_estimate=pl.CostEstimate(flops=13_000_000_000, bytes_accessed=1_500_000, transcendentals=2_700_000),
    )(logit_scale, logit_bias, image_features, proj_weight, text_embed, text_match.reshape(1, rows))


def solution(mesh):
    return jax.shard_map(
        local,
        mesh=mesh,
        in_specs=(P("mp", "dp"), P("mp", None), P(("dp", "mp"), None), P(("dp", "mp")), P(), P()),
        out_specs=(P(("dp", "mp"), None), P("mp", "dp"), P("mp", None)),
        check_vma=False,
    )
```

```python
import functools

import jax
import jax.numpy as jnp
from jax import lax
from jax.experimental import pallas as pl
from jax.experimental.pallas import tpu as pltpu
from jax.sharding import PartitionSpec as P

MESH = pl.DeviceIdType.MESH
norm_floor = 1e-06
f32, bf16 = jnp.float32, jnp.bfloat16

ZS, XS = 8, 4
ROWS = 72
PAD = 80
BLOCK = 144
HEAD = 80
NEAR = 64
GROUP = 1152
EMBED = 1152
CHUNK = 288
TILE = 384
TEXT_ORDER = (0, -1, 1, -2, 2, -3, 3, 4)
TEXT_POS = {step: at for at, step in enumerate(TEXT_ORDER)}
IMAGE_ORDER = (2, 1, 3, 0)
PIECES, PIECE_ROWS, PIECE_COLS = 15, 16, 384
SEMS = 160


def inverse_norm(values):
    return lax.rsqrt(jnp.sum(values * values, axis=1, keepdims=True) + norm_floor)


def norm_backward(values, inverse, upstream):
    along = jnp.sum(values * upstream, axis=1, keepdims=True)
    return inverse * upstream - inverse * inverse * inverse * along * values


def kernel(
    scale_ref, bias_ref, f_ref, w_ref, t_ref, m_ref,
    tg_ref, fg_ref, pg_ref,
    xsend, xrecv, fw, tsend, trecv, msend, mrecv, tn, mt, mcol, proj, unit, logits, coef, dt, du,
    tout, tra, tlb, tr, tl, ysend_t, yrecv_t,
    csend, crecv, xout, xra, xlb, xr, xl, yout, yin, mine_sum, gp,
    ws, wr, wa,
    send_sem, recv_sem,
):
    d, m = lax.axis_index("dp"), lax.axis_index("mp")
    z, yhi = d // 2, d % 2
    x, ylo, core = m // 4, (m // 2) % 2, m % 2

    def at_z(step):
        return {"dp": lax.rem(z + step + ZS, ZS) * 2 + yhi, "mp": m}

    def at_x(step):
        return {"dp": d, "mp": lax.rem(x + step + XS, XS) * 4 + ylo * 2 + core}

    other_yhi = {"dp": z * 2 + (1 - yhi), "mp": m}
    other_ylo = {"dp": d, "mp": x * 4 + (1 - ylo) * 2 + core}
    sibling = {"dp": d, "mp": x * 4 + ylo * 2 + (1 - core)}

    def dp_at(index):
        return {"dp": index, "mp": m}

    barrier = pltpu.get_barrier_semaphore()
    partners = [sibling, other_ylo, other_yhi, at_x(1), at_x(-1), at_z(1), at_z(-1)]
    for partner in partners:
        pl.semaphore_signal(barrier, inc=1, device_id=partner, device_id_type=MESH)

    keys = {}

    def key(name):
        return keys.setdefault(name, len(keys))

    def describe(name, src, dst, target):
        k = key(name)
        return pltpu.make_async_remote_copy(
            src_ref=src, dst_ref=dst, send_sem=send_sem.at[k], recv_sem=recv_sem.at[k],
            device_id=target, device_id_type=MESH,
        )

    sent = []

    def start(name, src, dst, target):
        copy = describe(name, src, dst, target)
        copy.start()
        sent.append(copy)

    def arrived(name, dst, target=sibling):
        describe(name, dst, dst, target).wait_recv()

    f_mine, w_mine = f_ref[...].astype(f32), w_ref[...].astype(f32)
    is_first = core == 0
    pad_rows = jnp.zeros((PAD - ROWS, EMBED), f32)
    xsend[...] = jnp.concatenate([jnp.where(is_first, w_mine, f_mine), pad_rows]).astype(bf16)
    text_values = t_ref[...].astype(f32)
    text_inverse = inverse_norm(text_values)
    text_mine = text_values * text_inverse
    tsend[...] = jnp.concatenate([text_mine, pad_rows]).astype(bf16)
    msend[...] = jnp.zeros_like(msend)
    msend[0:1, 0:ROWS] = m_ref[...]
    pl.semaphore_wait(barrier, len(partners))

    start("x0", xsend, xrecv, sibling)

    def text_rows(step, part):
        first = TEXT_POS[step] * BLOCK
        return pl.ds(first, NEAR) if part == 0 else pl.ds(first + NEAR, BLOCK - NEAR)

    def text_forward(step, part, way, new_step):
        start(("t", new_step, part), tn.at[text_rows(step, part)], tn.at[text_rows(new_step, part)], at_z(way))
        if part == 1:
            start(("m", new_step), mt.at[TEXT_POS[step]], mt.at[TEXT_POS[new_step]], at_z(way))

    def text_arrived(step, part):
        arrived(("t", step, part), tn.at[text_rows(step, part)])
        if part == 1:
            arrived(("m", step), mt.at[TEXT_POS[step]])

    tn[pl.ds(0, NEAR), :] = text_mine[:NEAR].astype(bf16)
    text_forward(0, 0, 1, -1)
    text_forward(0, 0, -1, 1)
    start("t0", tsend, trecv, other_yhi)
    start("m0", msend, mrecv, other_yhi)

    def slot(index, count=1):
        return pl.ds(index * BLOCK, count * BLOCK)

    def mine(index):
        return fw.at[core, slot(index)]

    def share(index):
        start(("fs", index), mine(index), mine(index), sibling)

    own = jnp.where(is_first, f_mine, w_mine)
    arrived("x0", xrecv)
    theirs = xrecv[...].astype(f32)[:ROWS]
    fw[core, slot(0), :] = jnp.concatenate(
        [jnp.where(is_first, own, theirs), jnp.where(is_first, theirs, own)]
    ).astype(bf16)
    start(("fx", 1), mine(0), mine(1), other_ylo)
    start(("fx", 4), mine(0), mine(4), at_x(1))
    start(("fx", 2), mine(0), mine(2), at_x(-1))
    share(0)

    arrived("t0", trecv)
    arrived("m0", mrecv)
    theirs = trecv[...].astype(f32)[:ROWS]
    tn[text_rows(0, 1), :] = jnp.concatenate([tsend[...].astype(f32)[NEAR:ROWS], theirs]).astype(bf16)
    mt[0, 0:1, :] = msend[0:1, :]
    mt[0, 1:2, :] = mrecv[0:1, :]
    mt[0, 2:8, :] = jnp.zeros((6, 128), jnp.int32)
    text_forward(0, 1, 1, -1)
    text_forward(0, 1, -1, 1)

    def text_pass(step, part):
        for way in (1, -1):
            text_arrived(-way * step, part)
            text_forward(-way * step, part, way, -way * (step + 1))

    text_pass(1, 0)
    arrived(("fx", 1), mine(1))
    start(("fx", 5), mine(1), mine(5), at_x(1))
    start(("fx", 3), mine(1), mine(3), at_x(-1))
    share(1)
    arrived(("fx", 4), mine(4))
    start(("fx", 6), mine(4), mine(6), at_x(1))
    share(4)
    arrived(("fx", 2), mine(2))
    share(2)
    text_pass(1, 1)
    text_pass(2, 0)
    arrived(("fx", 3), mine(3))
    start(("fx", 7), mine(3), mine(7), at_x(-1))
    share(3)
    arrived(("fx", 5), mine(5))
    share(5)
    text_pass(2, 1)
    text_arrived(-3, 0)
    text_forward(-3, 0, 1, 4)
    arrived(("fx", 6), mine(6))
    share(6)
    arrived(("fx", 7), mine(7))
    share(7)
    text_arrived(3, 0)
    text_arrived(3, 1)
    text_forward(3, 1, -1, 4)
    for index in range(8):
        arrived(("fs", index), fw.at[1 - core, slot(index)])

    def project(tile, _):
        columns = pl.ds(pl.multiple_of(tile * TILE, TILE), TILE)
        values = lax.dot_general(
            fw[0, :, columns], fw[1], (((0,), (0,)), ((), ())), preferred_element_type=f32
        )
        normal = (values * inverse_norm(values)).astype(bf16)
        for part in range(TILE // 96):
            piece = tile * (TILE // 96) + part
            away = lax.rem(piece // 3 - x + XS, XS)
            place = jnp.where(away == 2, 0, jnp.where(away == 1, 1, jnp.where(away == 3, 2, 3)))
            row = pl.multiple_of(place * CHUNK + (piece % 3) * 96, 96)
            proj[pl.ds(row, 96), :] = values[part * 96:(part + 1) * 96]
            unit[pl.ds(row, 96), :] = normal[part * 96:(part + 1) * 96]
        return 0

    lax.fori_loop(0, GROUP // TILE, project, 0)

    lane = lax.broadcasted_iota(jnp.int32, (1, GROUP), 1)
    image_index = jnp.zeros_like(lane)
    for place, away in enumerate(IMAGE_ORDER):
        base = d * GROUP + lax.rem(x + away, XS) * CHUNK - place * CHUNK
        image_index = jnp.where(lane // CHUNK == place, base + lane, image_index)

    row_number = lax.broadcasted_iota(jnp.int32, (ROWS, 128), 0)

    def columns_of(step):
        place = TEXT_POS[step]
        from_z = lax.rem(z + step + ZS, ZS)
        for which, high in enumerate((yhi, 1 - yhi)):
            row = mt[place, which:which + 1, :]
            column = jnp.transpose(jnp.broadcast_to(row, (128, 128)))[:ROWS]
            rows = pl.ds(place * BLOCK + which * ROWS, ROWS)
            mcol[0, rows, :] = column
            mcol[1, rows, :] = ((from_z * 2 + high) * 16 + m) * ROWS + row_number

    log2e = 1.4426950408889634
    scaling = scale_ref[0]
    slope, shift = scaling * log2e, bias_ref[0] * log2e

    def coefficients_of(chunk):
        for step in TEXT_ORDER[2 * chunk:2 * chunk + 2]:
            columns_of(step)
        rows = pl.ds(chunk * CHUNK, CHUNK)
        logits[...] = lax.dot_general(
            tn[rows, :], unit[...], (((1,), (1,)), ((), ())), preferred_element_type=f32
        )

        def coefficients(step, _):
            at = pl.multiple_of(step * 16, 16)
            here = pl.ds(chunk * CHUNK + at, 16)
            match = mcol[0, here, 0:1]
            index = mcol[1, here, 0:1]
            positive = (index == image_index) | (match == image_index)
            power = slope * logits[pl.ds(at, 16), :] + shift
            grown = 1.0 + jnp.exp2(jnp.where(positive, power, -power))
            coef[here, :] = (
                jnp.where(positive, -scaling, scaling) * pl.reciprocal(grown, approx=True)
            ).astype(bf16)
            return 0

        lax.fori_loop(0, CHUNK // 16, coefficients, 0)

    coefficients_of(0)
    coefficients_of(1)
    text_arrived(-3, 1)
    coefficients_of(2)
    text_arrived(4, 0)
    text_arrived(4, 1)
    coefficients_of(3)

    parts = ((0, HEAD), (HEAD, BLOCK - HEAD))

    def image_tile(tile):
        columns = pl.ds(tile * TILE, TILE)
        du[columns, :] = lax.dot_general(
            coef[:, columns], tn[...], (((0,), (0,)), ((), ())), preferred_element_type=f32
        )

    def text_tile(chunk):
        rows = pl.ds(chunk * CHUNK, CHUNK)
        dt[rows, :] = jnp.dot(coef[rows, :], unit[...], preferred_element_type=f32)

    def image_block(place, which, first=0, count=BLOCK):
        return pl.ds(pl.multiple_of(place * CHUNK + which * BLOCK + first, 16), count)

    def to_sibling(place):
        csend[place] = du[image_block(place, 1 - core), :].astype(bf16)
        start(("c", place), csend.at[place], crecv.at[place], sibling)

    def with_sibling(place, part):
        first, count = parts[part]
        return du[image_block(place, core, first, count), :] + crecv[place, pl.ds(first, count), :].astype(f32)

    def image_send(place, part, way, buffer, extra=None):
        first, count = parts[part]
        values = with_sibling(place, part)
        if extra is not None:
            values = values + extra
        xout[place, pl.ds(first, count), :] = values.astype(bf16)
        there = buffer.at[pl.ds(first, count)] if buffer.shape[0] == BLOCK else buffer
        start(("x", place, part, way), xout.at[place, pl.ds(first, count)], there, at_x(way))

    def image_arrived(place, part, way, buffer):
        first, count = parts[part]
        there = buffer.at[pl.ds(first, count)] if buffer.shape[0] == BLOCK else buffer
        arrived(("x", place, part, way), there)
        return there[...].astype(f32)

    def text_partial(step, part):
        first, count = parts[part]
        return dt[pl.ds(TEXT_POS[step] * BLOCK + first, count), :]

    def text_buffer(way, away, part):
        first, count = parts[part]
        if away == 4:
            return tra if way == 1 else tlb
        return (tr if way == 1 else tl).at[3 - away, pl.ds(first, count)]

    def text_came(way, away, part):
        there = text_buffer(way, away, part)
        arrived(("ts", way, away, part), there)
        return there[...].astype(f32)

    def text_send(way, away, part):
        first, count = parts[part]
        step = 4 if away == 4 else way * away
        values = text_partial(step, part)
        if away == 2 or away == 1 or (away == 3 and part == (0 if way == 1 else 1)):
            values = values + text_came(way, away + 1, part)
        place = TEXT_POS[step]
        tout[place, pl.ds(first, count), :] = values.astype(bf16)
        start(
            ("ts", way, away, part), tout.at[place, pl.ds(first, count)], text_buffer(way, away, part), at_z(way)
        )

    image_tile(0)
    to_sibling(0)
    image_tile(1)
    to_sibling(1)
    arrived(("c", 0), crecv.at[0])
    image_send(0, 0, 1, xra)
    image_send(0, 1, -1, xlb)
    image_tile(2)
    to_sibling(2)
    to_sibling(3)
    arrived(("c", 1), crecv.at[1])
    image_send(1, 1, 1, xr)
    text_tile(3)
    text_send(1, 4, 0)
    text_send(-1, 4, 1)
    arrived(("c", 2), crecv.at[2])
    image_send(2, 0, -1, xl)
    text_send(1, 3, 1)
    text_tile(2)
    text_send(-1, 3, 0)
    image_send(1, 0, 1, xr, image_arrived(0, 0, 1, xra))
    image_send(2, 1, -1, xl, image_arrived(0, 1, -1, xlb))
    text_tile(1)
    text_tile(0)
    text_send(1, 3, 0)
    text_send(-1, 3, 1)
    arrived(("c", 3), crecv.at[3])

    def gp_block(from_x, which, part=None):
        first, count = (0, BLOCK) if part is None else parts[part]
        return gp.at[pl.ds(pl.multiple_of(from_x * CHUNK + which * BLOCK + first, 16), count)]

    owner = ylo == core
    not_owner = jnp.logical_not(owner)
    text_send(1, 2, 1)
    text_send(-1, 2, 0)

    def to_owner(part):
        rows = pl.ds(*parts[part])
        return describe(("yo", part), yout.at[rows], yin.at[rows], other_ylo)

    def from_owner(part):
        block = gp_block(x, core, part)
        return describe(("yg", part), block, block, other_ylo)

    for part in range(2):
        rows = pl.ds(*parts[part])
        mine_sum[rows, :] = (
            with_sibling(3, part) + image_arrived(1, part, 1, xr) + image_arrived(2, part, -1, xl)
        )

        @pl.when(not_owner)
        def _(rows=rows, part=part):
            yout[rows, :] = mine_sum[rows, :].astype(bf16)
            to_owner(part).start()

    text_send(1, 2, 0)
    text_send(-1, 2, 1)

    for part in range(2):
        @pl.when(owner)
        def _(part=part):
            first, count = parts[part]
            to_owner(part).wait_recv()
            total = mine_sum[pl.ds(first, count), :] + yin[pl.ds(first, count), :].astype(f32)
            projected = proj[image_block(3, core, first, count), :]
            place = pl.multiple_of(x * CHUNK + core * BLOCK + first, 16)
            gp[pl.ds(place, count), :] = norm_backward(
                projected, inverse_norm(projected), total
            ).astype(bf16)
            from_owner(part).start()

        @pl.when(not_owner)
        def _(part=part):
            from_owner(part).wait_recv()

        block = gp_block(x, core, part)
        start(("gr", part), block, block, at_x(1))
        start(("gl", part), block, block, at_x(-1))
        start(("gs", 0, part), block, block, sibling)

    left_x, right_x, far_x = lax.rem(x + 3, XS), lax.rem(x + 1, XS), lax.rem(x + 2, XS)

    def gp_share(index, from_x, part):
        block = gp_block(from_x, core, part)
        start(("gs", index, part), block, block, sibling)

    text_send(1, 1, 1)
    text_send(-1, 1, 0)
    block = gp_block(left_x, core, 0)
    arrived(("gr", 0), block)
    start("gfr", block, block, at_x(1))
    gp_share(1, left_x, 0)
    arrived(("gl", 0), gp_block(right_x, core, 0))
    gp_share(2, right_x, 0)
    block = gp_block(right_x, core, 1)
    arrived(("gl", 1), block)
    start("gfl", block, block, at_x(-1))
    gp_share(2, right_x, 1)
    arrived(("gr", 1), gp_block(left_x, core, 1))
    gp_share(1, left_x, 1)
    text_send(1, 1, 0)
    text_send(-1, 1, 1)
    arrived("gfr", gp_block(far_x, core, 0))
    gp_share(3, far_x, 0)
    arrived("gfl", gp_block(far_x, core, 1))
    gp_share(3, far_x, 1)

    total = jnp.concatenate(
        [text_partial(0, part) + text_came(1, 1, part) + text_came(-1, 1, part) for part in range(2)]
    )
    ysend_t[...] = jnp.concatenate([total[ROWS:], pad_rows]).astype(bf16)
    start("ty", ysend_t, yrecv_t, other_yhi)

    for part in range(2):
        for index, from_x in enumerate((x, left_x, right_x, far_x)):
            arrived(("gs", index, part), gp_block(from_x, 1 - core, part))

    part = jnp.dot(f_ref[...], gp[...], preferred_element_type=f32)
    ws[...] = jnp.concatenate([part, pad_rows]).astype(bf16)

    def piece_of(index):
        rows = pl.ds(pl.multiple_of((index // 3) * PIECE_ROWS, PIECE_ROWS), PIECE_ROWS)
        columns = pl.ds(pl.multiple_of((index % 3) * PIECE_COLS, PIECE_COLS), PIECE_COLS)
        return rows, columns

    def numbered(base, to, source, src, dst, target):
        return pltpu.make_async_remote_copy(
            src_ref=src, dst_ref=dst, send_sem=send_sem.at[base + to], recv_sem=recv_sem.at[base + source],
            device_id=target, device_id_type=MESH,
        )

    base = len(keys)
    again = base + 16

    def scatter(index):
        rows, columns = piece_of(index)
        return numbered(base, index, d, ws.at[rows, columns], wr.at[d], dp_at(index))

    def gather(index):
        return numbered(again, index, d, wa.at[d], wa.at[d], dp_at(index))

    for index in range(PIECES):
        @pl.when(d != index)
        def _(index=index):
            scatter(index).start()

    fg_ref[...] = lax.dot_general(
        w_ref[...], gp[...], (((1,), (1,)), ((), ())), preferred_element_type=f32
    ).astype(bf16)

    arrived("ty", yrecv_t)
    text_total = total[:ROWS] + yrecv_t[...].astype(f32)[:ROWS]
    tg_ref[...] = norm_backward(text_values, text_inverse, text_total).astype(bf16)

    @pl.when(d < PIECES)
    def _():
        rows, columns = piece_of(d)
        wr[d] = ws[rows, columns]
        for source in range(16):
            @pl.when(d != source)
            def _(source=source):
                numbered(base, 0, source, wr.at[source], wr.at[source], sibling).wait_recv()
        total = wr[0].astype(f32)
        for source in range(1, 16):
            total = total + wr[source].astype(f32)
        wa[d] = total.astype(bf16)
        for index in range(16):
            @pl.when(d != index)
            def _(index=index):
                gather(index).start()

    for index in range(PIECES):
        @pl.when(d != index)
        def _(index=index):
            numbered(again, 0, index, wa.at[index], wa.at[index], sibling).wait_recv()
    for index in range(PIECES):
        first = (index // 3) * PIECE_ROWS
        count = min(PIECE_ROWS, ROWS - first)
        columns = pl.ds((index % 3) * PIECE_COLS, PIECE_COLS)
        pg_ref[pl.ds(first, count), columns] = wa[index].astype(f32)[:count]

    for copy in sent:
        copy.wait_send()

    @pl.when(not_owner)
    def _():
        for part in range(2):
            to_owner(part).wait_send()

    @pl.when(owner)
    def _():
        for part in range(2):
            from_owner(part).wait_send()

    for index in range(PIECES):
        @pl.when(d != index)
        def _(index=index):
            scatter(index).wait_send()

    @pl.when(d < PIECES)
    def _():
        for index in range(16):
            @pl.when(d != index)
            def _(index=index):
                gather(index).wait_send()


def local(image_features, proj_weight, text_embed, text_match, logit_scale, logit_bias):
    vmem = pl.BlockSpec(memory_space=pltpu.VMEM)
    smem = pl.BlockSpec(memory_space=pltpu.SMEM)
    block = (BLOCK, EMBED)
    square = (GROUP, EMBED)
    tail = BLOCK - HEAD
    scratch = [
        pltpu.VMEM((PAD, EMBED), bf16),
        pltpu.VMEM((PAD, EMBED), bf16),
        pltpu.VMEM((2,) + square, bf16),
        pltpu.VMEM((PAD, EMBED), bf16),
        pltpu.VMEM((PAD, EMBED), bf16),
        pltpu.VMEM((8, 128), jnp.int32),
        pltpu.VMEM((8, 128), jnp.int32),
        pltpu.VMEM(square, bf16),
        pltpu.VMEM((8, 8, 128), jnp.int32),
        pltpu.VMEM((2, GROUP, 128), jnp.int32),
        pltpu.VMEM(square, f32),
        pltpu.VMEM(square, bf16),
        pltpu.VMEM((CHUNK, GROUP), f32),
        pltpu.VMEM(square, bf16),
        pltpu.VMEM(square, f32),
        pltpu.VMEM(square, f32),
        pltpu.VMEM((8,) + block, bf16),
        pltpu.VMEM((HEAD, EMBED), bf16),
        pltpu.VMEM((tail, EMBED), bf16),
        pltpu.VMEM((3,) + block, bf16),
        pltpu.VMEM((3,) + block, bf16),
        pltpu.VMEM((PAD, EMBED), bf16),
        pltpu.VMEM((PAD, EMBED), bf16),
        pltpu.VMEM((4,) + block, bf16),
        pltpu.VMEM((4,) + block, bf16),
        pltpu.VMEM((3,) + block, bf16),
        pltpu.VMEM((HEAD, EMBED), bf16),
        pltpu.VMEM((tail, EMBED), bf16),
        pltpu.VMEM(block, bf16),
        pltpu.VMEM(block, bf16),
        pltpu.VMEM(block, bf16),
        pltpu.VMEM(block, bf16),
        pltpu.VMEM(block, f32),
        pltpu.VMEM(square, bf16),
        pltpu.VMEM((PAD, EMBED), bf16),
        pltpu.VMEM((16, PIECE_ROWS, PIECE_COLS), bf16),
        pltpu.VMEM((16, PIECE_ROWS, PIECE_COLS), bf16),
        pltpu.SemaphoreType.DMA((SEMS,)),
        pltpu.SemaphoreType.DMA((SEMS,)),
    ]
    rows = text_embed.shape[0]
    return pl.pallas_call(
        kernel,
        out_shape=(
            jax.ShapeDtypeStruct((rows, EMBED), bf16),
            jax.ShapeDtypeStruct((rows, GROUP), bf16),
            jax.ShapeDtypeStruct((rows, EMBED), f32),
        ),
        in_specs=[smem, smem, vmem, vmem, vmem, vmem],
        out_specs=(vmem, vmem, vmem),
        scratch_shapes=scratch,
        compiler_params=pltpu.CompilerParams(
            collective_id=0, has_side_effects=True, vmem_limit_bytes=60 * 1024 * 1024
        ),
        cost_estimate=pl.CostEstimate(flops=13_000_000_000, bytes_accessed=1_500_000, transcendentals=2_700_000),
    )(logit_scale, logit_bias, image_features, proj_weight, text_embed, text_match.reshape(1, rows))


def solution(mesh):
    return jax.shard_map(
        local,
        mesh=mesh,
        in_specs=(P("mp", "dp"), P("mp", None), P(("dp", "mp"), None), P(("dp", "mp")), P(), P()),
        out_specs=(P(("dp", "mp"), None), P("mp", "dp"), P("mp", None)),
        check_vma=False,
    )
```

```python
import functools

import jax
import jax.numpy as jnp
from jax import lax
from jax.experimental import pallas as pl
from jax.experimental.pallas import tpu as pltpu
from jax.sharding import PartitionSpec as P

MESH = pl.DeviceIdType.MESH
norm_floor = 1e-06
f32, bf16 = jnp.float32, jnp.bfloat16

ZS, XS = 8, 4
ROWS = 72
PAD = 80
BLOCK = 144
HEAD = 80
NEAR = 64
GROUP = 1152
EMBED = 1152
CHUNK = 288
TILE = 384
TEXT_ORDER = (0, -1, 1, -2, 2, -3, 3, 4)
TEXT_POS = {step: at for at, step in enumerate(TEXT_ORDER)}
PIECES, PIECE_ROWS, PIECE_COLS = 15, 16, 384
SEMS = 224


def inverse_norm(values):
    return lax.rsqrt(jnp.sum(values * values, axis=1, keepdims=True) + norm_floor)


def norm_backward(values, inverse, upstream):
    along = jnp.sum(values * upstream, axis=1, keepdims=True)
    return inverse * upstream - inverse * inverse * inverse * along * values


def kernel(
    scale_ref, bias_ref, f_ref, w_ref, t_ref, m_ref,
    tg_ref, fg_ref, pg_ref,
    xsend, xrecv, wf, ff, tsend, trecv, msend, mrecv, tn, mt, mcol, proj, unit, logits, coef, dt, du,
    tout, tra, tlb, tr, tl, ysend_t, yrecv_t,
    csend, crecv, xout, xra, xlb, xr, xl, yout, yin, mine_sum, gp,
    ws, wr, wa,
    send_sem, recv_sem,
):
    d, m = lax.axis_index("dp"), lax.axis_index("mp")
    z, yhi = d // 2, d % 2
    x, ylo, core = m // 4, (m // 2) % 2, m % 2

    def at_z(step):
        return {"dp": lax.rem(z + step + ZS, ZS) * 2 + yhi, "mp": m}

    beside_x = {
        way: {"dp": d, "mp": lax.rem(x + way + XS, XS) * 4 + ylo * 2 + core} for way in (1, -1)
    }

    def at_x(way):
        return beside_x[way]

    other_yhi = {"dp": z * 2 + (1 - yhi), "mp": m}
    other_ylo = {"dp": d, "mp": x * 4 + (1 - ylo) * 2 + core}
    sibling = {"dp": d, "mp": x * 4 + ylo * 2 + (1 - core)}

    def dp_at(index):
        return {"dp": index, "mp": m}

    barrier = pltpu.get_barrier_semaphore()
    partners = [sibling, other_ylo, other_yhi, at_x(1), at_x(-1), at_z(1), at_z(-1)]
    for partner in partners:
        pl.semaphore_signal(barrier, inc=1, device_id=partner, device_id_type=MESH)

    keys = {}

    def key(name):
        return keys.setdefault(name, len(keys))

    def describe(name, src, dst, target):
        k = key(name)
        return pltpu.make_async_remote_copy(
            src_ref=src, dst_ref=dst, send_sem=send_sem.at[k], recv_sem=recv_sem.at[k],
            device_id=target, device_id_type=MESH,
        )

    sent = {}

    def start(name, src, dst, target):
        copy = describe(name, src, dst, target)
        copy.start()
        sent[name] = lambda: copy

    def arrived(name, dst, target=sibling):
        describe(name, dst, dst, target).wait_recv()

    f_mine, w_mine = f_ref[...].astype(f32), w_ref[...].astype(f32)
    is_first = core == 0
    owner = ylo == core
    not_owner = jnp.logical_not(owner)
    left_x, right_x, far_x = lax.rem(x + 3, XS), lax.rem(x + 1, XS), lax.rem(x + 2, XS)
    parts = ((0, HEAD), (HEAD, BLOCK - HEAD))
    pad_rows = jnp.zeros((PAD - ROWS, EMBED), f32)
    xsend[0] = jnp.concatenate([w_mine, pad_rows]).astype(bf16)
    xsend[1] = jnp.concatenate([f_mine, pad_rows]).astype(bf16)
    text_values = t_ref[...].astype(f32)
    text_inverse = inverse_norm(text_values)
    text_mine = text_values * text_inverse
    tsend[...] = jnp.concatenate([text_mine, pad_rows]).astype(bf16)
    msend[...] = jnp.zeros_like(msend)
    msend[0:1, 0:ROWS] = m_ref[...]
    pl.semaphore_wait(barrier, len(partners))

    start("x0", xsend, xrecv, sibling)

    def text_rows(step, part):
        first = TEXT_POS[step] * BLOCK
        return pl.ds(first, NEAR) if part == 0 else pl.ds(first + NEAR, BLOCK - NEAR)

    def text_forward(step, part, way, new_step):
        start(("t", new_step, part), tn.at[text_rows(step, part)], tn.at[text_rows(new_step, part)], at_z(way))
        if part == 1:
            start(("m", new_step), mt.at[TEXT_POS[step]], mt.at[TEXT_POS[new_step]], at_z(way))

    def text_arrived(step, part):
        arrived(("t", step, part), tn.at[text_rows(step, part)])
        if part == 1:
            arrived(("m", step), mt.at[TEXT_POS[step]])

    tn[pl.ds(0, NEAR), :] = text_mine[:NEAR].astype(bf16)
    text_forward(0, 0, 1, -1)
    text_forward(0, 0, -1, 1)
    start("t0", tsend, trecv, other_yhi)
    start("m0", msend, mrecv, other_yhi)

    def block_rows(from_x, which, part=None):
        first, count = (0, BLOCK) if part is None else parts[part]
        return pl.ds(pl.multiple_of(from_x * CHUNK + which * BLOCK + first, 16), count)

    def block_of(name, from_x, which, part=None):
        rows = block_rows(from_x, which, part)
        return wf.at[rows] if name == "w" else ff.at[:, rows]

    def by_role(of_owner, of_other):
        pl.when(owner)(of_owner)
        pl.when(not_owner)(of_other)

    def by_core(run):
        for index in range(2):
            pl.when(core == index)(functools.partial(run, index))

    class Block:
        def __init__(self, name, what, from_x, which, target, halves=False):
            self.name, self.what, self.from_x, self.which = name, what, from_x, which
            self.target, self.halves = target, halves

        def describe(self, part=None, target=None):
            block = block_of(self.what, self.from_x, self.which, part)
            return describe(self.name, block, block, self.target if target is None else target)

        def run(self, method, mine=True):
            if self.halves:
                by_core(lambda index: getattr(self.describe(index if mine else 1 - index), method)())
            else:
                getattr(self.describe(), method)()

        def start(self):
            self.run("start")
            sent[self.name] = self

        def arrive(self, mine=True):
            self.run("wait_recv", mine)

        def wait_send(self):
            self.run("wait_send")

    way_x = lax.rem(x + 1 + 2 * core, XS)
    ahead = {"dp": d, "mp": way_x * 4 + ylo * 2 + core}
    behind_x = lax.rem(x + 3 + 2 * core, XS)
    other_behind_x = lax.rem(x + 1 + 2 * core, XS)
    other_y = 1 - ylo

    def w_pair(name, from_mine, from_theirs, which, target, halves):
        return Block(name, "w", from_mine, which, target, halves), Block(name, "w", from_theirs[0], from_theirs[1], target, halves)

    w_own, w_behind = w_pair("w1", x, (behind_x, ylo), ylo, ahead, False)
    w_on, w_far = w_pair("w2", behind_x, (far_x, ylo), ylo, ahead, True)
    y_own, y_own_in = w_pair("y0", x, (x, other_y), ylo, other_ylo, True)
    y_behind, y_behind_in = w_pair("y1", behind_x, (behind_x, other_y), ylo, other_ylo, False)
    y_far, y_far_in = w_pair("y2", far_x, (far_x, other_y), ylo, other_ylo, True)

    def w_share(name, from_x, which, halves):
        theirs = other_behind_x if not halves else from_x
        return w_pair(name, from_x, (theirs, which), which, sibling, halves)

    shares = {
        "s1": w_share("s1", behind_x, ylo, False),
        "s2": w_share("s2", far_x, ylo, True),
        "s3": w_share("s3", x, other_y, True),
        "s4": w_share("s4", behind_x, other_y, False),
        "s5": w_share("s5", far_x, other_y, True),
    }

    def same(kind, name, from_x, target, part=None):
        block = block_of(name, from_x, core, part)
        return describe((kind, name, part), block, block, target)

    def move(kind, name, from_x, target, part=None):
        same(kind, name, from_x, target, part).start()
        sent[(kind, name, part)] = functools.partial(same, kind, name, from_x, target, part)

    def came(kind, name, from_x, part=None):
        same(kind, name, from_x, sibling, part).wait_recv()

    tiles = GROUP // TILE
    gathered = ("f",)

    def spread(name):
        move("right", name, x, at_x(1))
        move("left", name, x, at_x(-1))

    def spread_other(name):
        same("across", name, x, other_ylo).wait_recv()
        spread(name)
        same("share", name, x, sibling).start()

    def far(name):
        came("right", name, left_x)
        move("far", name, left_x, at_x(1), 0)
        move("share_left", name, left_x, sibling)
        came("left", name, right_x)
        move("far", name, right_x, at_x(-1), 1)
        move("share_right", name, right_x, sibling)

    def finish(name):
        for part in range(2):
            came("far", name, far_x, part)
            move("share_far", name, far_x, sibling, part)

    def complete(name):
        for kind, from_x, part in (
            ("share_left", left_x, None), ("share_right", right_x, None),
            ("share_far", far_x, 0), ("share_far", far_x, 1),
        ):
            block = block_of(name, from_x, 1 - core, part)
            describe((kind, name, part), block, block, sibling).wait_recv()

        @pl.when(owner)
        def _():
            block = block_of(name, x, 1 - core)
            describe(("share", name, None), block, block, sibling).wait_recv()

    arrived("x0", xrecv)
    for index, own in enumerate((w_mine, f_mine)):
        theirs = xrecv[index].astype(f32)[:ROWS]
        packed = jnp.concatenate(
            [jnp.where(is_first, own, theirs), jnp.where(is_first, theirs, own)]
        ).astype(bf16)
        rows = block_rows(x, ylo)
        if index == 0:
            wf[rows, :] = packed
        else:
            for tile in range(tiles):
                ff[tile, rows, :] = packed[:, tile * TILE:(tile + 1) * TILE]

    w_own.start()

    @pl.when(owner)
    def _():
        same("across", "f", x, other_ylo).start()
        spread("f")

    y_own.start()

    def text_pass(step, part):
        for way in (1, -1):
            text_arrived(-way * step, part)
            text_forward(-way * step, part, way, -way * (step + 1))

    text_pass(1, 0)
    arrived("t0", trecv)
    arrived("m0", mrecv)
    theirs = trecv[...].astype(f32)[:ROWS]
    tn[text_rows(0, 1), :] = jnp.concatenate([tsend[...].astype(f32)[NEAR:ROWS], theirs]).astype(bf16)
    mt[0, 0:1, :] = msend[0:1, :]
    mt[0, 1:2, :] = mrecv[0:1, :]
    mt[0, 2:8, :] = jnp.zeros((6, 128), jnp.int32)
    text_forward(0, 1, 1, -1)
    text_forward(0, 1, -1, 1)

    row_number = lax.broadcasted_iota(jnp.int32, (ROWS, 128), 0)

    def columns_of(step):
        place = TEXT_POS[step]
        from_z = lax.rem(z + step + ZS, ZS)
        for which, high in enumerate((yhi, 1 - yhi)):
            row = mt[place, which:which + 1, :]
            column = jnp.transpose(jnp.broadcast_to(row, (128, 128)))[:ROWS]
            rows = pl.ds(place * BLOCK + which * ROWS, ROWS)
            mcol[0, rows, :] = column
            mcol[1, rows, :] = ((from_z * 2 + high) * 16 + m) * ROWS + row_number

    w_behind.arrive()
    w_on.start()
    y_behind.start()
    shares["s1"][0].start()
    by_role(functools.partial(far, "f"), functools.partial(spread_other, "f"))
    columns_of(0)
    text_pass(2, 0)
    y_own_in.arrive()
    shares["s3"][0].start()
    text_pass(1, 1)
    w_far.arrive()
    y_far.start()
    shares["s2"][0].start()
    by_role(functools.partial(finish, "f"), functools.partial(far, "f"))
    columns_of(-1)
    columns_of(1)
    text_arrived(-3, 0)
    text_forward(-3, 0, 1, 4)
    y_behind_in.arrive()
    shares["s4"][0].start()
    text_pass(2, 1)
    text_arrived(3, 0)
    columns_of(-2)
    columns_of(2)
    pl.when(not_owner)(functools.partial(finish, "f"))
    y_far_in.arrive()
    shares["s5"][0].start()
    complete("f")
    for name in ("s1", "s2", "s3", "s4", "s5"):
        shares[name][1].arrive(mine=False)
    text_arrived(3, 1)
    text_forward(3, 1, -1, 4)

    def project(tile):
        proj[pl.ds(tile * TILE, TILE), :] = lax.dot_general(
            ff[tile], wf[...], (((0,), (0,)), ((), ())), preferred_element_type=f32
        )

    def normalize(tile):
        for first in range(tile * TILE, (tile + 1) * TILE, 48):
            rows = pl.ds(first, 48)
            values = proj[rows, :]
            unit[rows, :] = (values * inverse_norm(values)).astype(bf16)

    log2e = 1.4426950408889634
    scaling = scale_ref[0]
    slope, shift = scaling * log2e, bias_ref[0] * log2e

    def products_of(buffer, chunk, tile):
        logits[buffer] = lax.dot_general(
            tn[pl.ds(chunk * CHUNK, CHUNK), :], unit[pl.ds(pl.multiple_of(tile * TILE, TILE), TILE), :],
            (((1,), (1,)), ((), ())), preferred_element_type=f32,
        )

    def signs_of(buffer, chunk, tile):
        images = pl.ds(pl.multiple_of(tile * TILE, TILE), TILE)
        image_index = d * GROUP + tile * TILE + lax.broadcasted_iota(jnp.int32, (1, TILE), 1)
        count = 16
        for at in range(0, CHUNK, count):
            here = pl.ds(chunk * CHUNK + at, count)
            match = jnp.concatenate([mcol[0, here, :]] * (TILE // 128), axis=1)
            index = jnp.concatenate([mcol[1, here, :]] * (TILE // 128), axis=1)
            positive = (index == image_index) | (match == image_index)
            power = slope * logits[buffer, pl.ds(at, count), :] + shift
            grown = 1.0 + jnp.exp2(jnp.where(positive, power, -power))
            coef[here, images] = (
                jnp.where(positive, -scaling, scaling) * pl.reciprocal(grown, approx=True)
            ).astype(bf16)

    def coefficients_of(*units):
        for at, unit_at in enumerate(units):
            if at == 0:
                products_of(0, *unit_at)
            if at + 1 < len(units):
                products_of((at + 1) % 2, *units[at + 1])
            signs_of(at % 2, *unit_at)

    project(0)
    project(1)
    normalize(0)
    project(2)
    normalize(1)
    normalize(2)
    coefficients_of((0, 0), (0, 1), (0, 2), (1, 0), (1, 1), (1, 2))
    text_arrived(-3, 1)
    columns_of(-3)
    coefficients_of((2, 0), (2, 1), (2, 2))
    text_arrived(4, 0)
    text_arrived(4, 1)
    columns_of(3)
    columns_of(4)

    def image_tile(tile):
        columns = pl.ds(pl.multiple_of(tile * TILE, TILE), TILE)
        du[columns, :] = lax.dot_general(
            coef[:, columns], tn[...], (((0,), (0,)), ((), ())), preferred_element_type=f32
        )

    def text_tile(chunk):
        rows = pl.ds(chunk * CHUNK, CHUNK)
        dt[rows, :] = jnp.dot(coef[rows, :], unit[...], preferred_element_type=f32)

    image_x = (far_x, right_x, left_x, x)

    def image_block(place, which, first=0, count=BLOCK):
        return pl.ds(pl.multiple_of(image_x[place] * CHUNK + which * BLOCK + first, 16), count)

    def to_sibling(place):
        csend[place] = du[image_block(place, 1 - core), :].astype(bf16)
        start(("c", place), csend.at[place], crecv.at[place], sibling)

    def with_sibling(place, part):
        first, count = parts[part]
        return du[image_block(place, core, first, count), :] + crecv[place, pl.ds(first, count), :].astype(f32)

    def image_send(place, part, way, buffer, extra=None):
        first, count = parts[part]
        values = with_sibling(place, part)
        if extra is not None:
            values = values + extra
        xout[place, pl.ds(first, count), :] = values.astype(bf16)
        there = buffer.at[pl.ds(first, count)] if buffer.shape[0] == BLOCK else buffer
        start(("x", place, part, way), xout.at[place, pl.ds(first, count)], there, at_x(way))

    def image_arrived(place, part, way, buffer):
        first, count = parts[part]
        there = buffer.at[pl.ds(first, count)] if buffer.shape[0] == BLOCK else buffer
        arrived(("x", place, part, way), there)
        return there[...].astype(f32)

    def text_partial(step, part):
        first, count = parts[part]
        return dt[pl.ds(TEXT_POS[step] * BLOCK + first, count), :]

    def text_buffer(way, away, part):
        first, count = parts[part]
        if away == 4:
            return tra if way == 1 else tlb
        return (tr if way == 1 else tl).at[3 - away, pl.ds(first, count)]

    def text_came(way, away, part):
        there = text_buffer(way, away, part)
        arrived(("ts", way, away, part), there)
        return there[...].astype(f32)

    def text_send(way, away, part):
        first, count = parts[part]
        step = 4 if away == 4 else way * away
        values = text_partial(step, part)
        if away == 2 or away == 1 or (away == 3 and part == (0 if way == 1 else 1)):
            values = values + text_came(way, away + 1, part)
        place = TEXT_POS[step]
        tout[place, pl.ds(first, count), :] = values.astype(bf16)
        start(
            ("ts", way, away, part), tout.at[place, pl.ds(first, count)], text_buffer(way, away, part), at_z(way)
        )

    first_tile = jnp.where(far_x < 2, 0, 2)
    products_of(0, 3, first_tile)
    products_of(1, 3, 1)
    signs_of(0, 3, first_tile)
    products_of(0, 3, 2 - first_tile)
    signs_of(1, 3, 1)
    image_tile(first_tile)
    signs_of(0, 3, 2 - first_tile)
    image_tile(1)
    to_sibling(0)
    image_tile(2 - first_tile)
    arrived(("c", 0), crecv.at[0])
    image_send(0, 0, 1, xra)
    image_send(0, 1, -1, xlb)
    to_sibling(1)
    to_sibling(2)
    to_sibling(3)
    arrived(("c", 1), crecv.at[1])
    image_send(1, 1, 1, xr)
    text_tile(3)
    text_send(1, 4, 0)
    text_send(-1, 4, 1)
    arrived(("c", 2), crecv.at[2])
    image_send(2, 0, -1, xl)
    text_send(1, 3, 1)
    text_tile(2)
    text_send(-1, 3, 0)
    image_send(1, 0, 1, xr, image_arrived(0, 0, 1, xra))
    image_send(2, 1, -1, xl, image_arrived(0, 1, -1, xlb))
    text_tile(1)
    text_tile(0)
    text_send(1, 3, 0)
    text_send(-1, 3, 1)
    arrived(("c", 3), crecv.at[3])

    def gp_block(from_x, which, part=None):
        first, count = (0, BLOCK) if part is None else parts[part]
        return gp.at[pl.ds(pl.multiple_of(from_x * CHUNK + which * BLOCK + first, 16), count)]

    text_send(1, 2, 1)
    text_send(-1, 2, 0)

    def to_owner(part):
        rows = pl.ds(*parts[part])
        return describe(("yo", part), yout.at[rows], yin.at[rows], other_ylo)

    def from_owner(part):
        block = gp_block(x, core, part)
        return describe(("yg", part), block, block, other_ylo)

    for part in range(2):
        rows = pl.ds(*parts[part])
        mine_sum[rows, :] = (
            with_sibling(3, part) + image_arrived(1, part, 1, xr) + image_arrived(2, part, -1, xl)
        )

        @pl.when(not_owner)
        def _(rows=rows, part=part):
            yout[rows, :] = mine_sum[rows, :].astype(bf16)
            to_owner(part).start()

    text_send(1, 2, 0)
    text_send(-1, 2, 1)

    for part in range(2):
        @pl.when(owner)
        def _(part=part):
            first, count = parts[part]
            to_owner(part).wait_recv()
            total = mine_sum[pl.ds(first, count), :] + yin[pl.ds(first, count), :].astype(f32)
            projected = proj[image_block(3, core, first, count), :]
            place = pl.multiple_of(x * CHUNK + core * BLOCK + first, 16)
            gp[pl.ds(place, count), :] = norm_backward(
                projected, inverse_norm(projected), total
            ).astype(bf16)
            from_owner(part).start()

        @pl.when(not_owner)
        def _(part=part):
            from_owner(part).wait_recv()

        block = gp_block(x, core, part)
        start(("gr", part), block, block, at_x(1))
        start(("gl", part), block, block, at_x(-1))
        start(("gs", 0, part), block, block, sibling)

    def gp_share(index, from_x, part):
        block = gp_block(from_x, core, part)
        start(("gs", index, part), block, block, sibling)

    text_send(1, 1, 1)
    text_send(-1, 1, 0)
    block = gp_block(left_x, core, 0)
    arrived(("gr", 0), block)
    start("gfr", block, block, at_x(1))
    gp_share(1, left_x, 0)
    arrived(("gl", 0), gp_block(right_x, core, 0))
    gp_share(2, right_x, 0)
    block = gp_block(right_x, core, 1)
    arrived(("gl", 1), block)
    start("gfl", block, block, at_x(-1))
    gp_share(2, right_x, 1)
    arrived(("gr", 1), gp_block(left_x, core, 1))
    gp_share(1, left_x, 1)
    text_send(1, 1, 0)
    text_send(-1, 1, 1)
    arrived("gfr", gp_block(far_x, core, 0))
    gp_share(3, far_x, 0)
    arrived("gfl", gp_block(far_x, core, 1))
    gp_share(3, far_x, 1)

    total = jnp.concatenate(
        [text_partial(0, part) + text_came(1, 1, part) + text_came(-1, 1, part) for part in range(2)]
    )
    ysend_t[...] = jnp.concatenate([total[ROWS:], pad_rows]).astype(bf16)
    start("ty", ysend_t, yrecv_t, other_yhi)

    for part in range(2):
        for index, from_x in enumerate((x, left_x, right_x, far_x)):
            arrived(("gs", index, part), gp_block(from_x, 1 - core, part))

    part = jnp.dot(f_ref[...], gp[...], preferred_element_type=f32)
    ws[...] = jnp.concatenate([part, pad_rows]).astype(bf16)

    def piece_of(index):
        rows = pl.ds(pl.multiple_of((index // 3) * PIECE_ROWS, PIECE_ROWS), PIECE_ROWS)
        columns = pl.ds(pl.multiple_of((index % 3) * PIECE_COLS, PIECE_COLS), PIECE_COLS)
        return rows, columns

    def numbered(base, to, source, src, dst, target):
        return pltpu.make_async_remote_copy(
            src_ref=src, dst_ref=dst, send_sem=send_sem.at[base + to], recv_sem=recv_sem.at[base + source],
            device_id=target, device_id_type=MESH,
        )

    base = len(keys)
    again = base + 16

    def scatter(index):
        rows, columns = piece_of(index)
        return numbered(base, index, d, ws.at[rows, columns], wr.at[d], dp_at(index))

    def gather(index):
        return numbered(again, index, d, wa.at[d], wa.at[d], dp_at(index))

    for index in range(PIECES):
        @pl.when(d != index)
        def _(index=index):
            scatter(index).start()

    fg_ref[...] = lax.dot_general(
        w_ref[...], gp[...], (((1,), (1,)), ((), ())), preferred_element_type=f32
    ).astype(bf16)

    arrived("ty", yrecv_t)
    text_total = total[:ROWS] + yrecv_t[...].astype(f32)[:ROWS]
    tg_ref[...] = norm_backward(text_values, text_inverse, text_total).astype(bf16)

    @pl.when(d < PIECES)
    def _():
        rows, columns = piece_of(d)
        wr[d] = ws[rows, columns]
        for source in range(16):
            @pl.when(d != source)
            def _(source=source):
                numbered(base, 0, source, wr.at[source], wr.at[source], sibling).wait_recv()
        total = wr[0].astype(f32)
        for source in range(1, 16):
            total = total + wr[source].astype(f32)
        wa[d] = total.astype(bf16)
        for index in range(16):
            @pl.when(d != index)
            def _(index=index):
                gather(index).start()

    for index in range(PIECES):
        @pl.when(d != index)
        def _(index=index):
            numbered(again, 0, index, wa.at[index], wa.at[index], sibling).wait_recv()
    for index in range(PIECES):
        first = (index // 3) * PIECE_ROWS
        count = min(PIECE_ROWS, ROWS - first)
        columns = pl.ds((index % 3) * PIECE_COLS, PIECE_COLS)
        pg_ref[pl.ds(first, count), columns] = wa[index].astype(f32)[:count]

    for copy in sent.values():
        (copy if isinstance(copy, Block) else copy()).wait_send()

    @pl.when(not_owner)
    def _():
        for part in range(2):
            to_owner(part).wait_send()
        for name in gathered:
            same("share", name, x, sibling).wait_send()

    @pl.when(owner)
    def _():
        for part in range(2):
            from_owner(part).wait_send()
        for name in gathered:
            same("across", name, x, other_ylo).wait_send()

    for index in range(PIECES):
        @pl.when(d != index)
        def _(index=index):
            scatter(index).wait_send()

    @pl.when(d < PIECES)
    def _():
        for index in range(16):
            @pl.when(d != index)
            def _(index=index):
                gather(index).wait_send()


def local(image_features, proj_weight, text_embed, text_match, logit_scale, logit_bias):
    vmem = pl.BlockSpec(memory_space=pltpu.VMEM)
    smem = pl.BlockSpec(memory_space=pltpu.SMEM)
    block = (BLOCK, EMBED)
    square = (GROUP, EMBED)
    tail = BLOCK - HEAD
    scratch = [
        pltpu.VMEM((2, PAD, EMBED), bf16),
        pltpu.VMEM((2, PAD, EMBED), bf16),
        pltpu.VMEM(square, bf16),
        pltpu.VMEM((GROUP // TILE, GROUP, TILE), bf16),
        pltpu.VMEM((PAD, EMBED), bf16),
        pltpu.VMEM((PAD, EMBED), bf16),
        pltpu.VMEM((8, 128), jnp.int32),
        pltpu.VMEM((8, 128), jnp.int32),
        pltpu.VMEM(square, bf16),
        pltpu.VMEM((8, 8, 128), jnp.int32),
        pltpu.VMEM((2, GROUP, 128), jnp.int32),
        pltpu.VMEM(square, f32),
        pltpu.VMEM(square, bf16),
        pltpu.VMEM((2, CHUNK, TILE), f32),
        pltpu.VMEM(square, bf16),
        pltpu.VMEM(square, f32),
        pltpu.VMEM(square, f32),
        pltpu.VMEM((8,) + block, bf16),
        pltpu.VMEM((HEAD, EMBED), bf16),
        pltpu.VMEM((tail, EMBED), bf16),
        pltpu.VMEM((3,) + block, bf16),
        pltpu.VMEM((3,) + block, bf16),
        pltpu.VMEM((PAD, EMBED), bf16),
        pltpu.VMEM((PAD, EMBED), bf16),
        pltpu.VMEM((4,) + block, bf16),
        pltpu.VMEM((4,) + block, bf16),
        pltpu.VMEM((3,) + block, bf16),
        pltpu.VMEM((HEAD, EMBED), bf16),
        pltpu.VMEM((tail, EMBED), bf16),
        pltpu.VMEM(block, bf16),
        pltpu.VMEM(block, bf16),
        pltpu.VMEM(block, bf16),
        pltpu.VMEM(block, bf16),
        pltpu.VMEM(block, f32),
        pltpu.VMEM(square, bf16),
        pltpu.VMEM((PAD, EMBED), bf16),
        pltpu.VMEM((16, PIECE_ROWS, PIECE_COLS), bf16),
        pltpu.VMEM((16, PIECE_ROWS, PIECE_COLS), bf16),
        pltpu.SemaphoreType.DMA((SEMS,)),
        pltpu.SemaphoreType.DMA((SEMS,)),
    ]
    rows = text_embed.shape[0]
    return pl.pallas_call(
        kernel,
        out_shape=(
            jax.ShapeDtypeStruct((rows, EMBED), bf16),
            jax.ShapeDtypeStruct((rows, GROUP), bf16),
            jax.ShapeDtypeStruct((rows, EMBED), f32),
        ),
        in_specs=[smem, smem, vmem, vmem, vmem, vmem],
        out_specs=(vmem, vmem, vmem),
        scratch_shapes=scratch,
        compiler_params=pltpu.CompilerParams(
            collective_id=0, has_side_effects=True, vmem_limit_bytes=60 * 1024 * 1024
        ),
        cost_estimate=pl.CostEstimate(flops=13_000_000_000, bytes_accessed=1_500_000, transcendentals=2_700_000),
    )(logit_scale, logit_bias, image_features, proj_weight, text_embed, text_match.reshape(1, rows))


def solution(mesh):
    return jax.shard_map(
        local,
        mesh=mesh,
        in_specs=(P("mp", "dp"), P("mp", None), P(("dp", "mp"), None), P(("dp", "mp")), P(), P()),
        out_specs=(P(("dp", "mp"), None), P("mp", "dp"), P("mp", None)),
        check_vma=False,
    )
```

```python
import functools

import jax
import jax.numpy as jnp
from jax import lax
from jax.experimental import pallas as pl
from jax.experimental.pallas import tpu as pltpu
from jax.sharding import PartitionSpec as P

MESH = pl.DeviceIdType.MESH
norm_floor = 1e-06
f32, bf16 = jnp.float32, jnp.bfloat16

ZS, XS = 8, 4
ROWS = 72
PAD = 80
BLOCK = 144
HEAD = 80
TEXT_PARTS = ((0, 64), (64, 48), (112, 32))
FIRST = 48
GROUP = 1152
EMBED = 1152
CHUNK = 288
TILE = 384
TEXT_ORDER = (0, -1, 1, -2, 2, -3, 3, 4)
TEXT_POS = {step: at for at, step in enumerate(TEXT_ORDER)}
PIECES, PIECE_ROWS, PIECE_COLS = 15, 16, 384
SEMS = 192


def inverse_norm(values):
    return lax.rsqrt(jnp.sum(values * values, axis=1, keepdims=True) + norm_floor)


def norm_backward(values, inverse, upstream):
    along = jnp.sum(values * upstream, axis=1, keepdims=True)
    return inverse * upstream - inverse * inverse * inverse * along * values


def kernel(
    scale_ref, bias_ref, f_in, w_in, t_in, m_in,
    tg_out, fg_out, pg_out,
    f_ref, w_ref, t_ref, m_ref, tg_ref, fg_ref, pg_ref,
    xsend, xrecv, wf, ff, tsend, trecv, msend, mrecv, tn, mt, mcol, proj, unit, logits, coef, dt, du,
    tout, tra, tlb, tr, tl, ysend_t, yrecv_t,
    csend, crecv, xout, xra, xlb, xr, xl, yout, yin, mine_sum, gp,
    ws, wr, wa,
    send_sem, recv_sem, local_sem,
):
    loads = [
        pltpu.make_async_copy(source, held, local_sem.at[at])
        for at, (source, held) in enumerate(((t_in, t_ref), (w_in, w_ref), (f_in, f_ref), (m_in, m_ref)))
    ]
    for load in loads:
        load.start()

    def store(at, held, target):
        return pltpu.make_async_copy(held, target, local_sem.at[4 + at])

    d, m = lax.axis_index("dp"), lax.axis_index("mp")
    z, yhi = d // 2, d % 2
    x, ylo, core = m // 4, (m // 2) % 2, m % 2

    def at_z(step):
        return {"dp": lax.rem(z + step + ZS, ZS) * 2 + yhi, "mp": m}

    beside_x = {
        way: {"dp": d, "mp": lax.rem(x + way + XS, XS) * 4 + ylo * 2 + core} for way in (1, -1)
    }

    def at_x(way):
        return beside_x[way]

    other_yhi = {"dp": z * 2 + (1 - yhi), "mp": m}
    other_ylo = {"dp": d, "mp": x * 4 + (1 - ylo) * 2 + core}
    sibling = {"dp": d, "mp": x * 4 + ylo * 2 + (1 - core)}

    def dp_at(index):
        return {"dp": index, "mp": m}

    barrier = pltpu.get_barrier_semaphore()
    partners = [sibling, other_ylo, other_yhi, at_x(1), at_x(-1), at_z(1), at_z(-1)]
    for partner in partners:
        pl.semaphore_signal(barrier, inc=1, device_id=partner, device_id_type=MESH)

    keys = {}

    def key(name):
        return keys.setdefault(name, len(keys))

    def describe(name, src, dst, target):
        k = key(name)
        return pltpu.make_async_remote_copy(
            src_ref=src, dst_ref=dst, send_sem=send_sem.at[k], recv_sem=recv_sem.at[k],
            device_id=target, device_id_type=MESH,
        )

    sent = {}

    def start(name, src, dst, target):
        copy = describe(name, src, dst, target)
        copy.start()
        sent[name] = lambda: copy

    def arrived(name, dst, target=sibling):
        describe(name, dst, dst, target).wait_recv()

    for load in loads:
        load.wait()
    f_mine, w_mine = f_ref[...].astype(f32), w_ref[...].astype(f32)
    is_first = core == 0
    owner = ylo == core
    not_owner = jnp.logical_not(owner)
    left_x, right_x, far_x = lax.rem(x + 3, XS), lax.rem(x + 1, XS), lax.rem(x + 2, XS)
    parts = ((0, HEAD), (HEAD, BLOCK - HEAD))
    pad_rows = jnp.zeros((PAD - ROWS, EMBED), f32)
    xsend[0] = jnp.concatenate([w_mine, pad_rows]).astype(bf16)
    xsend[1] = jnp.concatenate([f_mine, pad_rows]).astype(bf16)
    text_values = t_ref[...].astype(f32)
    text_inverse = inverse_norm(text_values)
    text_mine = text_values * text_inverse
    tsend[...] = jnp.concatenate([text_mine, pad_rows]).astype(bf16)
    msend[...] = jnp.zeros_like(msend)
    msend[0:1, 0:ROWS] = m_ref[...]
    pl.semaphore_wait(barrier, len(partners))

    start("x0", xsend, xrecv, sibling)

    def text_rows(step, part):
        first, count = TEXT_PARTS[part]
        return pl.ds(TEXT_POS[step] * BLOCK + first, count)

    def text_forward(step, part, way, new_step):
        start(("t", new_step, part), tn.at[text_rows(step, part)], tn.at[text_rows(new_step, part)], at_z(way))
        if part == 2:
            start(("m", new_step), mt.at[TEXT_POS[step]], mt.at[TEXT_POS[new_step]], at_z(way))

    def text_arrived(step, part):
        arrived(("t", step, part), tn.at[text_rows(step, part)])
        if part == 2:
            arrived(("m", step), mt.at[TEXT_POS[step]])

    near = TEXT_PARTS[0][1]
    tn[pl.ds(0, near), :] = text_mine[:near].astype(bf16)
    text_forward(0, 0, 1, -1)
    text_forward(0, 0, -1, 1)
    start("t0", tsend.at[pl.ds(0, FIRST)], trecv.at[pl.ds(0, FIRST)], other_yhi)
    start("t1", tsend.at[pl.ds(FIRST, PAD - FIRST)], trecv.at[pl.ds(FIRST, PAD - FIRST)], other_yhi)
    start("m0", msend, mrecv, other_yhi)

    def block_rows(from_x, which, part=None):
        first, count = (0, BLOCK) if part is None else parts[part]
        return pl.ds(pl.multiple_of(from_x * CHUNK + which * BLOCK + first, 16), count)

    def block_of(name, from_x, which, part=None):
        rows = block_rows(from_x, which, part)
        return wf.at[rows] if name == "w" else ff.at[:, rows]

    def by_role(of_owner, of_other):
        pl.when(owner)(of_owner)
        pl.when(not_owner)(of_other)

    def by_core(run):
        for index in range(2):
            pl.when(core == index)(functools.partial(run, index))

    class Block:
        def __init__(self, name, what, from_x, which, target, halves=False):
            self.name, self.what, self.from_x, self.which = name, what, from_x, which
            self.target, self.halves = target, halves

        def describe(self, part=None, target=None):
            block = block_of(self.what, self.from_x, self.which, part)
            return describe(self.name, block, block, self.target if target is None else target)

        def run(self, method, mine=True):
            if self.halves:
                by_core(lambda index: getattr(self.describe(index if mine else 1 - index), method)())
            else:
                getattr(self.describe(), method)()

        def start(self):
            self.run("start")
            sent[self.name] = self

        def arrive(self, mine=True):
            self.run("wait_recv", mine)

        def wait_send(self):
            self.run("wait_send")

    way_x = lax.rem(x + 1 + 2 * core, XS)
    ahead = {"dp": d, "mp": way_x * 4 + ylo * 2 + core}
    behind_x = lax.rem(x + 3 + 2 * core, XS)
    other_behind_x = lax.rem(x + 1 + 2 * core, XS)
    other_y = 1 - ylo

    def w_pair(name, from_mine, from_theirs, which, target, halves):
        return Block(name, "w", from_mine, which, target, halves), Block(name, "w", from_theirs[0], from_theirs[1], target, halves)

    w_own, w_behind = w_pair("w1", x, (behind_x, ylo), ylo, ahead, False)
    w_on, w_far = w_pair("w2", behind_x, (far_x, ylo), ylo, ahead, True)
    y_own, y_own_in = w_pair("y0", x, (x, other_y), ylo, other_ylo, True)
    y_behind, y_behind_in = w_pair("y1", behind_x, (behind_x, other_y), ylo, other_ylo, False)
    y_far, y_far_in = w_pair("y2", far_x, (far_x, other_y), ylo, other_ylo, True)

    def w_share(name, from_x, which, halves):
        theirs = other_behind_x if not halves else from_x
        return w_pair(name, from_x, (theirs, which), which, sibling, halves)

    shares = {
        "s1": w_share("s1", behind_x, ylo, False),
        "s2": w_share("s2", far_x, ylo, True),
        "s3": w_share("s3", x, other_y, True),
        "s4": w_share("s4", behind_x, other_y, False),
        "s5": w_share("s5", far_x, other_y, True),
    }

    def same(kind, name, from_x, target, part=None):
        block = block_of(name, from_x, core, part)
        return describe((kind, name, part), block, block, target)

    def move(kind, name, from_x, target, part=None):
        same(kind, name, from_x, target, part).start()
        sent[(kind, name, part)] = functools.partial(same, kind, name, from_x, target, part)

    def came(kind, name, from_x, part=None):
        same(kind, name, from_x, sibling, part).wait_recv()

    tiles = GROUP // TILE
    gathered = ("f",)

    def spread(name):
        move("right", name, x, at_x(1))
        move("left", name, x, at_x(-1))

    def spread_other(name):
        same("across", name, x, other_ylo).wait_recv()
        spread(name)
        same("share", name, x, sibling).start()

    def far(name):
        came("right", name, left_x)
        move("far", name, left_x, at_x(1), 0)
        move("share_left", name, left_x, sibling)
        came("left", name, right_x)
        move("far", name, right_x, at_x(-1), 1)
        move("share_right", name, right_x, sibling)

    def finish(name):
        for part in range(2):
            came("far", name, far_x, part)
            move("share_far", name, far_x, sibling, part)

    def complete(name):
        for kind, from_x, part in (
            ("share_left", left_x, None), ("share_right", right_x, None),
            ("share_far", far_x, 0), ("share_far", far_x, 1),
        ):
            block = block_of(name, from_x, 1 - core, part)
            describe((kind, name, part), block, block, sibling).wait_recv()

        @pl.when(owner)
        def _():
            block = block_of(name, x, 1 - core)
            describe(("share", name, None), block, block, sibling).wait_recv()

    arrived("x0", xrecv)
    for index, own in enumerate((w_mine, f_mine)):
        theirs = xrecv[index].astype(f32)[:ROWS]
        packed = jnp.concatenate(
            [jnp.where(is_first, own, theirs), jnp.where(is_first, theirs, own)]
        ).astype(bf16)
        rows = block_rows(x, ylo)
        if index == 0:
            wf[rows, :] = packed
        else:
            for tile in range(tiles):
                ff[tile, rows, :] = packed[:, tile * TILE:(tile + 1) * TILE]

    w_own.start()

    @pl.when(owner)
    def _():
        same("across", "f", x, other_ylo).start()
        spread("f")

    y_own.start()

    def text_pass(step, part):
        for way in (1, -1):
            text_arrived(-way * step, part)
            text_forward(-way * step, part, way, -way * (step + 1))

    text_pass(1, 0)
    arrived("t0", trecv.at[pl.ds(0, FIRST)])
    taken = TEXT_PARTS[1][1] - (ROWS - near)
    tn[text_rows(0, 1), :] = jnp.concatenate(
        [tsend[...].astype(f32)[near:ROWS], trecv[pl.ds(0, FIRST), :].astype(f32)[:taken]]
    ).astype(bf16)
    text_forward(0, 1, 1, -1)
    text_forward(0, 1, -1, 1)
    arrived("t1", trecv.at[pl.ds(FIRST, PAD - FIRST)])
    arrived("m0", mrecv)
    tn[text_rows(0, 2), :] = trecv[...].astype(f32)[taken:ROWS].astype(bf16)
    mt[0, 0:1, :] = msend[0:1, :]
    mt[0, 1:2, :] = mrecv[0:1, :]
    mt[0, 2:8, :] = jnp.zeros((6, 128), jnp.int32)
    text_forward(0, 2, 1, -1)
    text_forward(0, 2, -1, 1)

    row_number = lax.broadcasted_iota(jnp.int32, (ROWS, 128), 0)

    def columns_of(step):
        place = TEXT_POS[step]
        from_z = lax.rem(z + step + ZS, ZS)
        for which, high in enumerate((yhi, 1 - yhi)):
            row = mt[place, which:which + 1, :]
            column = jnp.transpose(jnp.broadcast_to(row, (128, 128)))[:ROWS]
            rows = pl.ds(place * BLOCK + which * ROWS, ROWS)
            mcol[0, rows, :] = column
            mcol[1, rows, :] = ((from_z * 2 + high) * 16 + m) * ROWS + row_number

    w_behind.arrive()
    w_on.start()
    y_behind.start()
    shares["s1"][0].start()
    by_role(functools.partial(far, "f"), functools.partial(spread_other, "f"))
    columns_of(0)
    text_pass(2, 0)
    y_own_in.arrive()
    shares["s3"][0].start()
    text_pass(1, 1)
    text_pass(1, 2)
    w_far.arrive()
    y_far.start()
    shares["s2"][0].start()
    text_arrived(-3, 0)
    text_forward(-3, 0, 1, 4)
    by_role(functools.partial(finish, "f"), functools.partial(far, "f"))
    columns_of(-1)
    columns_of(1)
    text_pass(2, 1)
    y_behind_in.arrive()
    shares["s4"][0].start()
    text_pass(2, 2)
    text_arrived(3, 0)
    columns_of(-2)
    columns_of(2)
    pl.when(not_owner)(functools.partial(finish, "f"))
    y_far_in.arrive()
    shares["s5"][0].start()
    text_arrived(3, 1)
    text_forward(3, 1, -1, 4)
    complete("f")
    for name in ("s1", "s2", "s3", "s4", "s5"):
        shares[name][1].arrive(mine=False)

    def project(tile):
        proj[pl.ds(tile * TILE, TILE), :] = lax.dot_general(
            ff[tile], wf[...], (((0,), (0,)), ((), ())), preferred_element_type=f32
        )

    def normalize(tile):
        for first in range(tile * TILE, (tile + 1) * TILE, 48):
            rows = pl.ds(first, 48)
            values = proj[rows, :]
            unit[rows, :] = (values * inverse_norm(values)).astype(bf16)

    log2e = 1.4426950408889634
    scaling = scale_ref[0]
    slope, shift = scaling * log2e, bias_ref[0] * log2e

    def products_of(buffer, chunk, tile):
        logits[buffer] = lax.dot_general(
            tn[pl.ds(chunk * CHUNK, CHUNK), :], unit[pl.ds(pl.multiple_of(tile * TILE, TILE), TILE), :],
            (((1,), (1,)), ((), ())), preferred_element_type=f32,
        )

    def signs_of(buffer, chunk, tile):
        images = pl.ds(pl.multiple_of(tile * TILE, TILE), TILE)
        image_index = d * GROUP + tile * TILE + lax.broadcasted_iota(jnp.int32, (1, TILE), 1)
        count = 16
        for at in range(0, CHUNK, count):
            here = pl.ds(chunk * CHUNK + at, count)
            match = jnp.concatenate([mcol[0, here, :]] * (TILE // 128), axis=1)
            index = jnp.concatenate([mcol[1, here, :]] * (TILE // 128), axis=1)
            positive = (index == image_index) | (match == image_index)
            power = slope * logits[buffer, pl.ds(at, count), :] + shift
            grown = 1.0 + jnp.exp2(jnp.where(positive, power, -power))
            coef[here, images] = (
                jnp.where(positive, -scaling, scaling) * pl.reciprocal(grown, approx=True)
            ).astype(bf16)

    def coefficients_of(*units):
        for at, unit_at in enumerate(units):
            if at == 0:
                products_of(0, *unit_at)
            if at + 1 < len(units):
                products_of((at + 1) % 2, *units[at + 1])
            signs_of(at % 2, *unit_at)

    project(0)
    text_arrived(3, 2)
    text_forward(3, 2, -1, 4)
    project(1)
    normalize(0)
    project(2)
    normalize(1)
    normalize(2)
    coefficients_of((0, 0), (0, 1), (0, 2), (1, 0), (1, 1), (1, 2))
    text_arrived(-3, 1)
    text_arrived(-3, 2)
    columns_of(-3)
    coefficients_of((2, 0), (2, 1), (2, 2))
    text_arrived(4, 0)
    text_arrived(4, 1)
    text_arrived(4, 2)
    columns_of(3)
    columns_of(4)

    def image_tile(tile):
        columns = pl.ds(pl.multiple_of(tile * TILE, TILE), TILE)
        du[columns, :] = lax.dot_general(
            coef[:, columns], tn[...], (((0,), (0,)), ((), ())), preferred_element_type=f32
        )

    def text_tile(chunk):
        rows = pl.ds(chunk * CHUNK, CHUNK)
        dt[rows, :] = jnp.dot(coef[rows, :], unit[...], preferred_element_type=f32)

    image_x = (far_x, right_x, left_x, x)

    def image_block(place, which, first=0, count=BLOCK):
        return pl.ds(pl.multiple_of(image_x[place] * CHUNK + which * BLOCK + first, 16), count)

    def to_sibling(place):
        csend[place] = du[image_block(place, 1 - core), :].astype(bf16)
        start(("c", place), csend.at[place], crecv.at[place], sibling)

    def with_sibling(place, part):
        first, count = parts[part]
        return du[image_block(place, core, first, count), :] + crecv[place, pl.ds(first, count), :].astype(f32)

    def image_send(place, part, way, buffer, extra=None):
        first, count = parts[part]
        values = with_sibling(place, part)
        if extra is not None:
            values = values + extra
        xout[place, pl.ds(first, count), :] = values.astype(bf16)
        there = buffer.at[pl.ds(first, count)] if buffer.shape[0] == BLOCK else buffer
        start(("x", place, part, way), xout.at[place, pl.ds(first, count)], there, at_x(way))

    def image_arrived(place, part, way, buffer):
        first, count = parts[part]
        there = buffer.at[pl.ds(first, count)] if buffer.shape[0] == BLOCK else buffer
        arrived(("x", place, part, way), there)
        return there[...].astype(f32)

    def text_partial(step, part):
        first, count = parts[part]
        return dt[pl.ds(TEXT_POS[step] * BLOCK + first, count), :]

    def text_buffer(way, away, part):
        first, count = parts[part]
        if away == 4:
            return tra if way == 1 else tlb
        return (tr if way == 1 else tl).at[3 - away, pl.ds(first, count)]

    def text_came(way, away, part):
        there = text_buffer(way, away, part)
        arrived(("ts", way, away, part), there)
        return there[...].astype(f32)

    def text_send(way, away, part):
        first, count = parts[part]
        step = 4 if away == 4 else way * away
        values = text_partial(step, part)
        if away == 2 or away == 1 or (away == 3 and part == (0 if way == 1 else 1)):
            values = values + text_came(way, away + 1, part)
        place = TEXT_POS[step]
        tout[place, pl.ds(first, count), :] = values.astype(bf16)
        start(
            ("ts", way, away, part), tout.at[place, pl.ds(first, count)], text_buffer(way, away, part), at_z(way)
        )

    first_tile = jnp.where(far_x < 2, 0, 2)
    products_of(0, 3, first_tile)
    products_of(1, 3, 1)
    signs_of(0, 3, first_tile)
    products_of(0, 3, 2 - first_tile)
    signs_of(1, 3, 1)
    image_tile(first_tile)
    signs_of(0, 3, 2 - first_tile)
    image_tile(1)
    to_sibling(0)
    image_tile(2 - first_tile)
    arrived(("c", 0), crecv.at[0])
    image_send(0, 0, 1, xra)
    image_send(0, 1, -1, xlb)
    to_sibling(1)
    to_sibling(2)
    to_sibling(3)
    arrived(("c", 1), crecv.at[1])
    image_send(1, 1, 1, xr)
    text_tile(3)
    text_send(1, 4, 0)
    text_send(-1, 4, 1)
    arrived(("c", 2), crecv.at[2])
    image_send(2, 0, -1, xl)
    text_send(1, 3, 1)
    text_tile(2)
    text_send(-1, 3, 0)
    image_send(1, 0, 1, xr, image_arrived(0, 0, 1, xra))
    image_send(2, 1, -1, xl, image_arrived(0, 1, -1, xlb))
    text_tile(1)
    text_tile(0)
    text_send(1, 3, 0)
    text_send(-1, 3, 1)
    arrived(("c", 3), crecv.at[3])

    text_send(1, 2, 1)
    text_send(-1, 2, 0)

    def to_owner(part):
        rows = pl.ds(*parts[part])
        return describe(("yo", part), yout.at[rows], yin.at[rows], other_ylo)

    for part in range(2):
        rows = pl.ds(*parts[part])
        mine_sum[rows, :] = (
            with_sibling(3, part) + image_arrived(1, part, 1, xr) + image_arrived(2, part, -1, xl)
        )

        @pl.when(not_owner)
        def _(rows=rows, part=part):
            yout[rows, :] = mine_sum[rows, :].astype(bf16)
            to_owner(part).start()

    text_send(1, 2, 0)
    text_send(-1, 2, 1)

    def gp_copy(kind, tile, from_x, target, part=None):
        block = gp.at[tile, block_rows(from_x, core, part)]
        return describe((kind, tile, part), block, block, target)

    def gp_move(kind, tile, from_x, target, part=None):
        gp_copy(kind, tile, from_x, target, part).start()
        sent[(kind, tile, part)] = functools.partial(gp_copy, kind, tile, from_x, target, part)

    def gp_came(kind, tile, from_x, part=None):
        gp_copy(kind, tile, from_x, sibling, part).wait_recv()

    def gp_spread(tile):
        gp_move("gr", tile, x, at_x(1))
        gp_move("gl", tile, x, at_x(-1))
        gp_move("gs", tile, x, sibling)

    @pl.when(owner)
    def _():
        for part in range(2):
            first, count = parts[part]
            to_owner(part).wait_recv()
            total = mine_sum[pl.ds(first, count), :] + yin[pl.ds(first, count), :].astype(f32)
            projected = proj[image_block(3, core, first, count), :]
            result = norm_backward(projected, inverse_norm(projected), total).astype(bf16)
            for tile in range(tiles):
                gp[tile, block_rows(x, core, part), :] = result[:, tile * TILE:(tile + 1) * TILE]
        for tile in range(tiles):
            gp_copy("yg", tile, x, other_ylo).start()
            gp_spread(tile)

    @pl.when(not_owner)
    def _():
        for tile in range(tiles):
            gp_copy("yg", tile, x, other_ylo).wait_recv()
            gp_spread(tile)

    def gp_far(tile):
        gp_came("gr", tile, left_x)
        gp_move("gf", tile, left_x, at_x(1), 0)
        gp_move("gs_left", tile, left_x, sibling)
        gp_came("gl", tile, right_x)
        gp_move("gf", tile, right_x, at_x(-1), 1)
        gp_move("gs_right", tile, right_x, sibling)

    def gp_finish(tile):
        for part in range(2):
            gp_came("gf", tile, far_x, part)
            gp_move("gs_far", tile, far_x, sibling, part)

    def gp_complete(tile):
        for kind, from_x, part in (
            ("gs", x, None), ("gs_left", left_x, None), ("gs_right", right_x, None),
            ("gs_far", far_x, 0), ("gs_far", far_x, 1),
        ):
            block = gp.at[tile, block_rows(from_x, 1 - core, part)]
            describe((kind, tile, part), block, block, sibling).wait_recv()

    text_send(1, 1, 1)
    text_send(-1, 1, 0)
    gp_far(0)
    gp_far(1)
    gp_finish(0)
    gp_far(2)
    text_send(1, 1, 0)
    text_send(-1, 1, 1)

    def piece_of(index):
        rows = pl.ds(pl.multiple_of((index // 3) * PIECE_ROWS, PIECE_ROWS), PIECE_ROWS)
        columns = pl.ds(pl.multiple_of((index % 3) * PIECE_COLS, PIECE_COLS), PIECE_COLS)
        return rows, columns

    def numbered(base, to, source, src, dst, target):
        return pltpu.make_async_remote_copy(
            src_ref=src, dst_ref=dst, send_sem=send_sem.at[base + to], recv_sem=recv_sem.at[base + source],
            device_id=target, device_id_type=MESH,
        )

    base = SEMS - 32
    again = SEMS - 16

    def scatter(index):
        rows, columns = piece_of(index)
        return numbered(base, index, d, ws.at[rows, columns], wr.at[d], dp_at(index))

    def gather(index):
        return numbered(again, index, d, wa.at[d], wa.at[d], dp_at(index))

    def weight_tile(tile):
        gp_complete(tile)
        part = jnp.dot(f_ref[...], gp[tile], preferred_element_type=f32)
        ws[:, tile * TILE:(tile + 1) * TILE] = jnp.concatenate([part, pad_rows[:, :TILE]]).astype(bf16)
        for index in range(tile, PIECES, tiles):
            @pl.when(d != index)
            def _(index=index):
                scatter(index).start()

    def reduce_piece():
        rows, columns = piece_of(d)
        wr[d] = ws[rows, columns]
        for source in range(16):
            @pl.when(d != source)
            def _(source=source):
                numbered(base, 0, source, wr.at[source], wr.at[source], sibling).wait_recv()
        total = wr[0].astype(f32)
        for source in range(1, 16):
            total = total + wr[source].astype(f32)
        wa[d] = total.astype(bf16)
        for index in range(16):
            @pl.when(d != index)
            def _(index=index):
                gather(index).start()

    weight_tile(0)
    gp_finish(1)
    gp_finish(2)
    weight_tile(1)

    weight_tile(2)
    pl.when((d < PIECES) & (d % 3 == 0))(reduce_piece)
    feature = lax.dot_general(
        w_ref[:, :TILE], gp[0], (((1,), (1,)), ((), ())), preferred_element_type=f32
    )
    for tile in range(1, tiles):
        feature = feature + lax.dot_general(
            w_ref[:, tile * TILE:(tile + 1) * TILE], gp[tile], (((1,), (1,)), ((), ())), preferred_element_type=f32
        )
    fg_ref[...] = feature.astype(bf16)
    store(1, fg_ref, fg_out).start()

    total = jnp.concatenate(
        [text_partial(0, part) + text_came(1, 1, part) + text_came(-1, 1, part) for part in range(2)]
    )
    ysend_t[...] = jnp.concatenate([total[ROWS:], pad_rows]).astype(bf16)
    start("ty", ysend_t, yrecv_t, other_yhi)

    pl.when((d < PIECES) & (d % 3 != 0))(reduce_piece)

    arrived("ty", yrecv_t)
    text_total = total[:ROWS] + yrecv_t[...].astype(f32)[:ROWS]
    tg_ref[...] = norm_backward(text_values, text_inverse, text_total).astype(bf16)
    store(0, tg_ref, tg_out).start()

    for index in range(PIECES):
        @pl.when(d != index)
        def _(index=index):
            numbered(again, 0, index, wa.at[index], wa.at[index], sibling).wait_recv()
    for index in range(PIECES):
        first = (index // 3) * PIECE_ROWS
        count = min(PIECE_ROWS, ROWS - first)
        columns = pl.ds((index % 3) * PIECE_COLS, PIECE_COLS)
        pg_ref[pl.ds(first, count), columns] = wa[index].astype(f32)[:count]

    store(2, pg_ref, pg_out).start()

    assert len(keys) <= SEMS - 32
    for copy in sent.values():
        (copy if isinstance(copy, Block) else copy()).wait_send()

    @pl.when(not_owner)
    def _():
        for part in range(2):
            to_owner(part).wait_send()
        for name in gathered:
            same("share", name, x, sibling).wait_send()

    @pl.when(owner)
    def _():
        for tile in range(tiles):
            gp_copy("yg", tile, x, other_ylo).wait_send()
        for name in gathered:
            same("across", name, x, other_ylo).wait_send()

    for index in range(PIECES):
        @pl.when(d != index)
        def _(index=index):
            scatter(index).wait_send()

    @pl.when(d < PIECES)
    def _():
        for index in range(16):
            @pl.when(d != index)
            def _(index=index):
                gather(index).wait_send()

    for at, (held, target) in enumerate(((tg_ref, tg_out), (fg_ref, fg_out), (pg_ref, pg_out))):
        store(at, held, target).wait()


def local(image_features, proj_weight, text_embed, text_match, logit_scale, logit_bias):
    anywhere = pl.BlockSpec(memory_space=pl.ANY)
    smem = pl.BlockSpec(memory_space=pltpu.SMEM)
    block = (BLOCK, EMBED)
    square = (GROUP, EMBED)
    tail = BLOCK - HEAD
    scratch = [
        pltpu.VMEM((ROWS, GROUP), bf16),
        pltpu.VMEM((ROWS, EMBED), bf16),
        pltpu.VMEM((ROWS, EMBED), bf16),
        pltpu.VMEM((1, ROWS), jnp.int32),
        pltpu.VMEM((ROWS, EMBED), bf16),
        pltpu.VMEM((ROWS, GROUP), bf16),
        pltpu.VMEM((ROWS, EMBED), f32),
        pltpu.VMEM((2, PAD, EMBED), bf16),
        pltpu.VMEM((2, PAD, EMBED), bf16),
        pltpu.VMEM(square, bf16),
        pltpu.VMEM((GROUP // TILE, GROUP, TILE), bf16),
        pltpu.VMEM((PAD, EMBED), bf16),
        pltpu.VMEM((PAD, EMBED), bf16),
        pltpu.VMEM((8, 128), jnp.int32),
        pltpu.VMEM((8, 128), jnp.int32),
        pltpu.VMEM(square, bf16),
        pltpu.VMEM((8, 8, 128), jnp.int32),
        pltpu.VMEM((2, GROUP, 128), jnp.int32),
        pltpu.VMEM(square, f32),
        pltpu.VMEM(square, bf16),
        pltpu.VMEM((2, CHUNK, TILE), f32),
        pltpu.VMEM(square, bf16),
        pltpu.VMEM(square, f32),
        pltpu.VMEM(square, f32),
        pltpu.VMEM((8,) + block, bf16),
        pltpu.VMEM((HEAD, EMBED), bf16),
        pltpu.VMEM((tail, EMBED), bf16),
        pltpu.VMEM((3,) + block, bf16),
        pltpu.VMEM((3,) + block, bf16),
        pltpu.VMEM((PAD, EMBED), bf16),
        pltpu.VMEM((PAD, EMBED), bf16),
        pltpu.VMEM((4,) + block, bf16),
        pltpu.VMEM((4,) + block, bf16),
        pltpu.VMEM((3,) + block, bf16),
        pltpu.VMEM((HEAD, EMBED), bf16),
        pltpu.VMEM((tail, EMBED), bf16),
        pltpu.VMEM(block, bf16),
        pltpu.VMEM(block, bf16),
        pltpu.VMEM(block, bf16),
        pltpu.VMEM(block, bf16),
        pltpu.VMEM(block, f32),
        pltpu.VMEM((GROUP // TILE, GROUP, TILE), bf16),
        pltpu.VMEM((PAD, EMBED), bf16),
        pltpu.VMEM((16, PIECE_ROWS, PIECE_COLS), bf16),
        pltpu.VMEM((16, PIECE_ROWS, PIECE_COLS), bf16),
        pltpu.SemaphoreType.DMA((SEMS,)),
        pltpu.SemaphoreType.DMA((SEMS,)),
        pltpu.SemaphoreType.DMA((7,)),
    ]
    rows = text_embed.shape[0]
    return pl.pallas_call(
        kernel,
        out_shape=(
            jax.ShapeDtypeStruct((rows, EMBED), bf16),
            jax.ShapeDtypeStruct((rows, GROUP), bf16),
            jax.ShapeDtypeStruct((rows, EMBED), f32),
        ),
        in_specs=[smem, smem, anywhere, anywhere, anywhere, anywhere],
        out_specs=(anywhere, anywhere, anywhere),
        scratch_shapes=scratch,
        compiler_params=pltpu.CompilerParams(
            collective_id=0, has_side_effects=True, vmem_limit_bytes=60 * 1024 * 1024
        ),
        cost_estimate=pl.CostEstimate(flops=13_000_000_000, bytes_accessed=1_500_000, transcendentals=2_700_000),
    )(logit_scale, logit_bias, image_features, proj_weight, text_embed, text_match.reshape(1, rows))


def solution(mesh):
    return jax.shard_map(
        local,
        mesh=mesh,
        in_specs=(P("mp", "dp"), P("mp", None), P(("dp", "mp"), None), P(("dp", "mp")), P(), P()),
        out_specs=(P(("dp", "mp"), None), P("mp", "dp"), P("mp", None)),
        check_vma=False,
    )
```

```python
import functools

import jax
import jax.numpy as jnp
from jax import lax
from jax.experimental import pallas as pl
from jax.experimental.pallas import tpu as pltpu
from jax.sharding import PartitionSpec as P

MESH = pl.DeviceIdType.MESH
norm_floor = 1e-06
f32, bf16 = jnp.float32, jnp.bfloat16

ZS, XS = 8, 4
ROWS = 72
PAD = 80
BLOCK = 144
HEAD = 80
TEXT_PARTS = ((0, 64), (64, 48), (112, 32))
FIRST = 48
GROUP = 1152
EMBED = 1152
CHUNK = 288
TILE = 384
PIECE = 96
TEXT_ORDER = (0, -1, 1, -2, 2, -3, 3, 4)
TEXT_POS = {step: at for at, step in enumerate(TEXT_ORDER)}
PIECES, PIECE_ROWS, PIECE_COLS = 15, 16, 384
SEMS = 192


def inverse_norm(values):
    return lax.rsqrt(jnp.sum(values * values, axis=1, keepdims=True) + norm_floor)


def norm_backward(values, inverse, upstream):
    along = jnp.sum(values * upstream, axis=1, keepdims=True)
    return inverse * upstream - inverse * inverse * inverse * along * values


def kernel(
    scale_ref, bias_ref, f_in, w_in, t_in, m_in,
    all_out,
    f_ref, w_ref, t_ref, m_ref, tg_ref, fg_ref, pg_ref,
    xsend, xrecv, wf, ff, tsend, trecv, msend, mrecv, tn, mt, mcol, proj, unit, logits, coef, dt, du,
    tout, tra, tlb, tr, tl, ysend_t, yrecv_t,
    csend, crecv, xout, xra, xlb, xr, xl, yout, yin, mine_sum, gp,
    ws, wr, wa,
    send_sem, recv_sem, local_sem,
):
    tg_out, fg_out, pg_out = (all_out.at[at] for at in range(3))
    loads = [
        pltpu.make_async_copy(source, held, local_sem.at[at])
        for at, (source, held) in enumerate(((t_in, t_ref), (w_in, w_ref), (f_in, f_ref), (m_in, m_ref)))
    ]
    for load in loads:
        load.start()

    def store(at, held, target):
        return pltpu.make_async_copy(held, target, local_sem.at[4 + at])

    d, m = lax.axis_index("dp"), lax.axis_index("mp")
    z, yhi = d // 2, d % 2
    x, ylo, core = m // 4, (m // 2) % 2, m % 2

    def at_z(step):
        return {"dp": lax.rem(z + step + ZS, ZS) * 2 + yhi, "mp": m}

    beside_x = {
        way: {"dp": d, "mp": lax.rem(x + way + XS, XS) * 4 + ylo * 2 + core} for way in (1, -1)
    }

    def at_x(way):
        return beside_x[way]

    other_yhi = {"dp": z * 2 + (1 - yhi), "mp": m}
    other_ylo = {"dp": d, "mp": x * 4 + (1 - ylo) * 2 + core}
    sibling = {"dp": d, "mp": x * 4 + ylo * 2 + (1 - core)}

    def dp_at(index):
        return {"dp": index, "mp": m}

    barrier = pltpu.get_barrier_semaphore()
    partners = [sibling, other_ylo, other_yhi, at_x(1), at_x(-1), at_z(1), at_z(-1)]
    for partner in partners:
        pl.semaphore_signal(barrier, inc=1, device_id=partner, device_id_type=MESH)

    keys = {}

    def key(name):
        return keys.setdefault(name, len(keys))

    def describe(name, src, dst, target):
        k = key(name)
        return pltpu.make_async_remote_copy(
            src_ref=src, dst_ref=dst, send_sem=send_sem.at[k], recv_sem=recv_sem.at[k],
            device_id=target, device_id_type=MESH,
        )

    sent = {}

    def start(name, src, dst, target):
        copy = describe(name, src, dst, target)
        copy.start()
        sent[name] = lambda: copy

    def arrived(name, dst, target=sibling):
        describe(name, dst, dst, target).wait_recv()

    for load in loads:
        load.wait()
    f_mine, w_mine = f_ref[...].astype(f32), w_ref[...].astype(f32)
    is_first = core == 0
    owner = ylo == core
    not_owner = jnp.logical_not(owner)
    left_x, right_x, far_x = lax.rem(x + 3, XS), lax.rem(x + 1, XS), lax.rem(x + 2, XS)
    parts = ((0, HEAD), (HEAD, BLOCK - HEAD))
    pad_rows = jnp.zeros((PAD - ROWS, EMBED), f32)
    xsend[0] = jnp.concatenate([w_mine, pad_rows]).astype(bf16)
    xsend[1] = jnp.concatenate([f_mine, pad_rows]).astype(bf16)
    text_values = t_ref[...].astype(f32)
    text_inverse = inverse_norm(text_values)
    text_mine = text_values * text_inverse
    tsend[...] = jnp.concatenate([text_mine, pad_rows]).astype(bf16)
    msend[...] = jnp.zeros_like(msend)
    msend[0:1, 0:ROWS] = m_ref[...]
    pl.semaphore_wait(barrier, len(partners))

    start("x0", xsend, xrecv, sibling)

    def text_rows(step, part):
        first, count = TEXT_PARTS[part]
        return pl.ds(TEXT_POS[step] * BLOCK + first, count)

    def text_forward(step, part, way, new_step):
        start(("t", new_step, part), tn.at[text_rows(step, part)], tn.at[text_rows(new_step, part)], at_z(way))
        if part == 2:
            start(("m", new_step), mt.at[TEXT_POS[step]], mt.at[TEXT_POS[new_step]], at_z(way))

    def text_arrived(step, part):
        arrived(("t", step, part), tn.at[text_rows(step, part)])
        if part == 2:
            arrived(("m", step), mt.at[TEXT_POS[step]])

    near = TEXT_PARTS[0][1]
    tn[pl.ds(0, near), :] = text_mine[:near].astype(bf16)
    text_forward(0, 0, 1, -1)
    text_forward(0, 0, -1, 1)
    start("t0", tsend.at[pl.ds(0, FIRST)], trecv.at[pl.ds(0, FIRST)], other_yhi)
    start("t1", tsend.at[pl.ds(FIRST, PAD - FIRST)], trecv.at[pl.ds(FIRST, PAD - FIRST)], other_yhi)
    start("m0", msend, mrecv, other_yhi)

    def block_rows(from_x, which, part=None):
        first, count = (0, BLOCK) if part is None else parts[part]
        return pl.ds(pl.multiple_of(from_x * CHUNK + which * BLOCK + first, 16), count)

    def block_of(name, from_x, which, part=None):
        rows = block_rows(from_x, which, part)
        return wf.at[rows] if name == "w" else ff.at[:, rows]

    def by_role(of_owner, of_other):
        pl.when(owner)(of_owner)
        pl.when(not_owner)(of_other)

    def by_core(run):
        for index in range(2):
            pl.when(core == index)(functools.partial(run, index))

    class Block:
        def __init__(self, name, what, from_x, which, target, halves=False):
            self.name, self.what, self.from_x, self.which = name, what, from_x, which
            self.target, self.halves = target, halves

        def describe(self, part=None, target=None):
            block = block_of(self.what, self.from_x, self.which, part)
            return describe(self.name, block, block, self.target if target is None else target)

        def run(self, method, mine=True):
            if self.halves:
                by_core(lambda index: getattr(self.describe(index if mine else 1 - index), method)())
            else:
                getattr(self.describe(), method)()

        def start(self):
            self.run("start")
            sent[self.name] = self

        def arrive(self, mine=True):
            self.run("wait_recv", mine)

        def wait_send(self):
            self.run("wait_send")

    way_x = lax.rem(x + 1 + 2 * core, XS)
    ahead = {"dp": d, "mp": way_x * 4 + ylo * 2 + core}
    behind_x = lax.rem(x + 3 + 2 * core, XS)
    other_behind_x = lax.rem(x + 1 + 2 * core, XS)
    other_y = 1 - ylo

    def w_pair(name, from_mine, from_theirs, which, target, halves):
        return Block(name, "w", from_mine, which, target, halves), Block(name, "w", from_theirs[0], from_theirs[1], target, halves)

    w_own, w_behind = w_pair("w1", x, (behind_x, ylo), ylo, ahead, False)
    w_on, w_far = w_pair("w2", behind_x, (far_x, ylo), ylo, ahead, True)
    y_own, y_own_in = w_pair("y0", x, (x, other_y), ylo, other_ylo, True)
    y_behind, y_behind_in = w_pair("y1", behind_x, (behind_x, other_y), ylo, other_ylo, False)
    y_far, y_far_in = w_pair("y2", far_x, (far_x, other_y), ylo, other_ylo, True)

    def w_share(name, from_x, which, halves):
        theirs = other_behind_x if not halves else from_x
        return w_pair(name, from_x, (theirs, which), which, sibling, halves)

    shares = {
        "s1": w_share("s1", behind_x, ylo, False),
        "s2": w_share("s2", far_x, ylo, True),
        "s3": w_share("s3", x, other_y, True),
        "s4": w_share("s4", behind_x, other_y, False),
        "s5": w_share("s5", far_x, other_y, True),
    }

    def same(kind, name, from_x, target, part=None):
        block = block_of(name, from_x, core, part)
        return describe((kind, name, part), block, block, target)

    def move(kind, name, from_x, target, part=None):
        same(kind, name, from_x, target, part).start()
        sent[(kind, name, part)] = functools.partial(same, kind, name, from_x, target, part)

    def came(kind, name, from_x, part=None):
        same(kind, name, from_x, sibling, part).wait_recv()

    tiles = GROUP // TILE
    gathered = ("f",)

    def spread(name):
        move("right", name, x, at_x(1))
        move("left", name, x, at_x(-1))

    def spread_other(name):
        same("across", name, x, other_ylo).wait_recv()
        spread(name)
        same("share", name, x, sibling).start()

    def far(name):
        came("right", name, left_x)
        move("far", name, left_x, at_x(1), 0)
        move("share_left", name, left_x, sibling)
        came("left", name, right_x)
        move("far", name, right_x, at_x(-1), 1)
        move("share_right", name, right_x, sibling)

    def finish(name):
        for part in range(2):
            came("far", name, far_x, part)
            move("share_far", name, far_x, sibling, part)

    def complete(name):
        for kind, from_x, part in (
            ("share_left", left_x, None), ("share_right", right_x, None),
            ("share_far", far_x, 0), ("share_far", far_x, 1),
        ):
            block = block_of(name, from_x, 1 - core, part)
            describe((kind, name, part), block, block, sibling).wait_recv()

        @pl.when(owner)
        def _():
            block = block_of(name, x, 1 - core)
            describe(("share", name, None), block, block, sibling).wait_recv()

    arrived("x0", xrecv)
    for index, own in enumerate((w_mine, f_mine)):
        theirs = xrecv[index].astype(f32)[:ROWS]
        packed = jnp.concatenate(
            [jnp.where(is_first, own, theirs), jnp.where(is_first, theirs, own)]
        ).astype(bf16)
        rows = block_rows(x, ylo)
        if index == 0:
            wf[rows, :] = packed
        else:
            for tile in range(tiles):
                ff[tile, rows, :] = packed[:, tile * TILE:(tile + 1) * TILE]

    w_own.start()

    @pl.when(owner)
    def _():
        same("across", "f", x, other_ylo).start()
        spread("f")

    y_own.start()

    def text_pass(step, part):
        for way in (1, -1):
            text_arrived(-way * step, part)
            text_forward(-way * step, part, way, -way * (step + 1))

    text_pass(1, 0)
    arrived("t0", trecv.at[pl.ds(0, FIRST)])
    taken = TEXT_PARTS[1][1] - (ROWS - near)
    tn[text_rows(0, 1), :] = jnp.concatenate(
        [tsend[...].astype(f32)[near:ROWS], trecv[pl.ds(0, FIRST), :].astype(f32)[:taken]]
    ).astype(bf16)
    text_forward(0, 1, 1, -1)
    text_forward(0, 1, -1, 1)
    arrived("t1", trecv.at[pl.ds(FIRST, PAD - FIRST)])
    arrived("m0", mrecv)
    tn[text_rows(0, 2), :] = trecv[...].astype(f32)[taken:ROWS].astype(bf16)
    mt[0, 0:1, :] = msend[0:1, :]
    mt[0, 1:2, :] = mrecv[0:1, :]
    mt[0, 2:8, :] = jnp.zeros((6, 128), jnp.int32)
    text_forward(0, 2, 1, -1)
    text_forward(0, 2, -1, 1)

    row_number = lax.broadcasted_iota(jnp.int32, (ROWS, 128), 0)

    def columns_of(step):
        place = TEXT_POS[step]
        from_z = lax.rem(z + step + ZS, ZS)
        for which, high in enumerate((yhi, 1 - yhi)):
            row = mt[place, which:which + 1, :]
            column = jnp.transpose(jnp.broadcast_to(row, (128, 128)))[:ROWS]
            rows = pl.ds(place * BLOCK + which * ROWS, ROWS)
            mcol[0, rows, :] = column
            mcol[1, rows, :] = ((from_z * 2 + high) * 16 + m) * ROWS + row_number

    w_behind.arrive()
    w_on.start()
    y_behind.start()
    shares["s1"][0].start()
    by_role(functools.partial(far, "f"), functools.partial(spread_other, "f"))
    columns_of(0)
    text_pass(2, 0)
    y_own_in.arrive()
    shares["s3"][0].start()
    text_pass(1, 1)
    text_pass(1, 2)
    w_far.arrive()
    y_far.start()
    shares["s2"][0].start()
    text_arrived(-3, 0)
    text_forward(-3, 0, 1, 4)
    by_role(functools.partial(finish, "f"), functools.partial(far, "f"))
    columns_of(-1)
    columns_of(1)
    text_pass(2, 1)
    y_behind_in.arrive()
    shares["s4"][0].start()
    text_pass(2, 2)
    text_arrived(3, 0)
    columns_of(-2)
    columns_of(2)
    pl.when(not_owner)(functools.partial(finish, "f"))
    y_far_in.arrive()
    shares["s5"][0].start()
    text_arrived(3, 1)
    text_forward(3, 1, -1, 4)
    complete("f")
    for name in ("s1", "s2", "s3", "s4", "s5"):
        shares[name][1].arrive(mine=False)

    def project(tile):
        values = lax.dot_general(ff[tile], wf[...], (((0,), (0,)), ((), ())), preferred_element_type=f32)
        normal = (values * inverse_norm(values)).astype(bf16)
        for part in range(TILE // PIECE):
            piece = tile * (TILE // PIECE) + part
            away = lax.rem(piece // (CHUNK // PIECE) - x + XS, XS)
            place = jnp.where(away == 2, 0, jnp.where(away == 1, 1, jnp.where(away == 3, 2, 3)))
            row = pl.multiple_of(place * CHUNK + (piece % (CHUNK // PIECE)) * PIECE, PIECE)
            proj[pl.ds(row, PIECE), :] = values[part * PIECE:(part + 1) * PIECE]
            unit[pl.ds(row, PIECE), :] = normal[part * PIECE:(part + 1) * PIECE]

    image_x = (far_x, right_x, left_x, x)
    lane = lax.broadcasted_iota(jnp.int32, (1, GROUP), 1)
    image_number = jnp.zeros_like(lane)
    for place, from_x in enumerate(image_x):
        first = d * GROUP + (from_x - place) * CHUNK
        image_number = jnp.where(lane // CHUNK == place, first + lane, image_number)

    log2e = 1.4426950408889634
    scaling = scale_ref[0]
    slope, shift = scaling * log2e, bias_ref[0] * log2e

    def products_of(buffer, chunk, tile):
        logits[buffer] = lax.dot_general(
            tn[pl.ds(chunk * CHUNK, CHUNK), :], unit[pl.ds(pl.multiple_of(tile * TILE, TILE), TILE), :],
            (((1,), (1,)), ((), ())), preferred_element_type=f32,
        )

    def signs_of(buffer, chunk, tile):
        images = pl.ds(pl.multiple_of(tile * TILE, TILE), TILE)
        image_index = image_number[:, tile * TILE:(tile + 1) * TILE]
        count = 16
        for at in range(0, CHUNK, count):
            here = pl.ds(chunk * CHUNK + at, count)
            match = jnp.concatenate([mcol[0, here, :]] * (TILE // 128), axis=1)
            index = jnp.concatenate([mcol[1, here, :]] * (TILE // 128), axis=1)
            positive = (index == image_index) | (match == image_index)
            power = slope * logits[buffer, pl.ds(at, count), :] + shift
            grown = 1.0 + jnp.exp2(jnp.where(positive, power, -power))
            coef[here, images] = (
                jnp.where(positive, -scaling, scaling) * pl.reciprocal(grown, approx=True)
            ).astype(bf16)

    def coefficients_of(*units):
        for at, unit_at in enumerate(units):
            if at == 0:
                products_of(0, *unit_at)
            if at + 1 < len(units):
                products_of((at + 1) % 2, *units[at + 1])
            signs_of(at % 2, *unit_at)

    project(0)
    text_arrived(3, 2)
    text_forward(3, 2, -1, 4)
    project(1)
    project(2)
    coefficients_of((0, 0), (0, 1), (0, 2), (1, 0), (1, 1), (1, 2))
    text_arrived(-3, 1)
    text_arrived(-3, 2)
    columns_of(-3)
    coefficients_of((2, 0), (2, 1), (2, 2))
    text_arrived(4, 0)
    text_arrived(4, 1)
    text_arrived(4, 2)
    columns_of(3)
    columns_of(4)

    def image_tile(tile):
        columns = pl.ds(pl.multiple_of(tile * TILE, TILE), TILE)
        du[columns, :] = lax.dot_general(
            coef[:, columns], tn[...], (((0,), (0,)), ((), ())), preferred_element_type=f32
        )

    def text_tile(chunk):
        rows = pl.ds(chunk * CHUNK, CHUNK)
        dt[rows, :] = jnp.dot(coef[rows, :], unit[...], preferred_element_type=f32)

    def image_block(place, which, first=0, count=BLOCK):
        return pl.ds(pl.multiple_of(place * CHUNK + which * BLOCK + first, 16), count)

    def to_sibling(place):
        csend[place] = du[image_block(place, 1 - core), :].astype(bf16)
        start(("c", place), csend.at[place], crecv.at[place], sibling)

    def with_sibling(place, part):
        first, count = parts[part]
        return du[image_block(place, core, first, count), :] + crecv[place, pl.ds(first, count), :].astype(f32)

    def image_send(place, part, way, buffer, extra=None):
        first, count = parts[part]
        values = with_sibling(place, part)
        if extra is not None:
            values = values + extra
        xout[place, pl.ds(first, count), :] = values.astype(bf16)
        there = buffer.at[pl.ds(first, count)] if buffer.shape[0] == BLOCK else buffer
        start(("x", place, part, way), xout.at[place, pl.ds(first, count)], there, at_x(way))

    def image_arrived(place, part, way, buffer):
        first, count = parts[part]
        there = buffer.at[pl.ds(first, count)] if buffer.shape[0] == BLOCK else buffer
        arrived(("x", place, part, way), there)
        return there[...].astype(f32)

    def text_partial(step, part):
        first, count = parts[part]
        return dt[pl.ds(TEXT_POS[step] * BLOCK + first, count), :]

    def text_buffer(way, away, part):
        first, count = parts[part]
        if away == 4:
            return tra if way == 1 else tlb
        return (tr if way == 1 else tl).at[3 - away, pl.ds(first, count)]

    def text_came(way, away, part):
        there = text_buffer(way, away, part)
        arrived(("ts", way, away, part), there)
        return there[...].astype(f32)

    def text_send(way, away, part):
        first, count = parts[part]
        step = 4 if away == 4 else way * away
        values = text_partial(step, part)
        if away == 2 or away == 1 or (away == 3 and part == (0 if way == 1 else 1)):
            values = values + text_came(way, away + 1, part)
        place = TEXT_POS[step]
        tout[place, pl.ds(first, count), :] = values.astype(bf16)
        start(
            ("ts", way, away, part), tout.at[place, pl.ds(first, count)], text_buffer(way, away, part), at_z(way)
        )

    products_of(0, 3, 0)
    products_of(1, 3, 1)
    signs_of(0, 3, 0)
    products_of(0, 3, 2)
    image_tile(0)
    to_sibling(0)
    signs_of(1, 3, 1)
    image_tile(1)
    to_sibling(1)
    arrived(("c", 0), crecv.at[0])
    image_send(0, 0, 1, xra)
    image_send(0, 1, -1, xlb)
    signs_of(0, 3, 2)
    image_tile(2)
    to_sibling(2)
    to_sibling(3)
    arrived(("c", 1), crecv.at[1])
    image_send(1, 1, 1, xr)
    text_tile(3)
    text_send(1, 4, 0)
    text_send(-1, 4, 1)
    arrived(("c", 2), crecv.at[2])
    image_send(2, 0, -1, xl)
    text_send(1, 3, 1)
    text_tile(2)
    text_send(-1, 3, 0)
    image_send(1, 0, 1, xr, image_arrived(0, 0, 1, xra))
    image_send(2, 1, -1, xl, image_arrived(0, 1, -1, xlb))
    text_tile(1)
    text_tile(0)
    text_send(1, 3, 0)
    text_send(-1, 3, 1)
    arrived(("c", 3), crecv.at[3])

    text_send(1, 2, 1)
    text_send(-1, 2, 0)

    def to_owner(part):
        rows = pl.ds(*parts[part])
        return describe(("yo", part), yout.at[rows], yin.at[rows], other_ylo)

    for part in range(2):
        rows = pl.ds(*parts[part])
        mine_sum[rows, :] = (
            with_sibling(3, part) + image_arrived(1, part, 1, xr) + image_arrived(2, part, -1, xl)
        )

        @pl.when(not_owner)
        def _(rows=rows, part=part):
            yout[rows, :] = mine_sum[rows, :].astype(bf16)
            to_owner(part).start()

    text_send(1, 2, 0)
    text_send(-1, 2, 1)

    def gp_copy(kind, tile, from_x, target, part=None):
        block = gp.at[tile, block_rows(from_x, core, part)]
        return describe((kind, tile, part), block, block, target)

    def gp_move(kind, tile, from_x, target, part=None):
        gp_copy(kind, tile, from_x, target, part).start()
        sent[(kind, tile, part)] = functools.partial(gp_copy, kind, tile, from_x, target, part)

    def gp_came(kind, tile, from_x, part=None):
        gp_copy(kind, tile, from_x, sibling, part).wait_recv()

    def gp_spread(tile):
        gp_move("gr", tile, x, at_x(1))
        gp_move("gl", tile, x, at_x(-1))
        gp_move("gs", tile, x, sibling)

    @pl.when(owner)
    def _():
        for part in range(2):
            first, count = parts[part]
            to_owner(part).wait_recv()
            total = mine_sum[pl.ds(first, count), :] + yin[pl.ds(first, count), :].astype(f32)
            projected = proj[image_block(3, core, first, count), :]
            result = norm_backward(projected, inverse_norm(projected), total).astype(bf16)
            for tile in range(tiles):
                gp[tile, block_rows(x, core, part), :] = result[:, tile * TILE:(tile + 1) * TILE]
        for tile in range(tiles):
            gp_copy("yg", tile, x, other_ylo).start()
            gp_spread(tile)

    @pl.when(not_owner)
    def _():
        for tile in range(tiles):
            gp_copy("yg", tile, x, other_ylo).wait_recv()
            gp_spread(tile)

    def gp_far(tile):
        gp_came("gr", tile, left_x)
        gp_move("gf", tile, left_x, at_x(1), 0)
        gp_move("gs_left", tile, left_x, sibling)
        gp_came("gl", tile, right_x)
        gp_move("gf", tile, right_x, at_x(-1), 1)
        gp_move("gs_right", tile, right_x, sibling)

    def gp_finish(tile):
        for part in range(2):
            gp_came("gf", tile, far_x, part)
            gp_move("gs_far", tile, far_x, sibling, part)

    def gp_complete(tile):
        for kind, from_x, part in (
            ("gs", x, None), ("gs_left", left_x, None), ("gs_right", right_x, None),
            ("gs_far", far_x, 0), ("gs_far", far_x, 1),
        ):
            block = gp.at[tile, block_rows(from_x, 1 - core, part)]
            describe((kind, tile, part), block, block, sibling).wait_recv()

    text_send(1, 1, 1)
    text_send(-1, 1, 0)
    gp_far(0)
    gp_far(1)
    gp_finish(0)
    gp_far(2)
    text_send(1, 1, 0)
    text_send(-1, 1, 1)

    def piece_of(index):
        rows = pl.ds(pl.multiple_of((index // 3) * PIECE_ROWS, PIECE_ROWS), PIECE_ROWS)
        columns = pl.ds(pl.multiple_of((index % 3) * PIECE_COLS, PIECE_COLS), PIECE_COLS)
        return rows, columns

    def numbered(base, to, source, src, dst, target):
        return pltpu.make_async_remote_copy(
            src_ref=src, dst_ref=dst, send_sem=send_sem.at[base + to], recv_sem=recv_sem.at[base + source],
            device_id=target, device_id_type=MESH,
        )

    base = SEMS - 32
    again = SEMS - 16

    def scatter(index):
        rows, columns = piece_of(index)
        return numbered(base, index, d, ws.at[rows, columns], wr.at[d], dp_at(index))

    def gather(index):
        return numbered(again, index, d, wa.at[d], wa.at[d], dp_at(index))

    def weight_tile(tile):
        gp_complete(tile)
        part = jnp.dot(f_ref[...], gp[tile], preferred_element_type=f32)
        ws[:, tile * TILE:(tile + 1) * TILE] = jnp.concatenate([part, pad_rows[:, :TILE]]).astype(bf16)
        for index in range(tile, PIECES, tiles):
            @pl.when(d != index)
            def _(index=index):
                scatter(index).start()

    def reduce_piece():
        rows, columns = piece_of(d)
        wr[d] = ws[rows, columns]
        for source in range(16):
            @pl.when(d != source)
            def _(source=source):
                numbered(base, 0, source, wr.at[source], wr.at[source], sibling).wait_recv()
        total = wr[0].astype(f32)
        for source in range(1, 16):
            total = total + wr[source].astype(f32)
        wa[d] = total.astype(bf16)
        for index in range(16):
            @pl.when(d != index)
            def _(index=index):
                gather(index).start()

    weight_tile(0)
    gp_finish(1)
    gp_finish(2)
    weight_tile(1)

    weight_tile(2)
    pl.when((d < PIECES) & (d % 3 == 0))(reduce_piece)
    feature = lax.dot_general(
        w_ref[:, :TILE], gp[0], (((1,), (1,)), ((), ())), preferred_element_type=f32
    )
    for tile in range(1, tiles):
        feature = feature + lax.dot_general(
            w_ref[:, tile * TILE:(tile + 1) * TILE], gp[tile], (((1,), (1,)), ((), ())), preferred_element_type=f32
        )
    fg_ref[...] = feature.astype(bf16)
    store(1, fg_ref, fg_out).start()

    total = jnp.concatenate(
        [text_partial(0, part) + text_came(1, 1, part) + text_came(-1, 1, part) for part in range(2)]
    )
    ysend_t[...] = jnp.concatenate([total[ROWS:], pad_rows]).astype(bf16)
    start("ty", ysend_t, yrecv_t, other_yhi)

    pl.when((d < PIECES) & (d % 3 != 0))(reduce_piece)

    arrived("ty", yrecv_t)
    text_total = total[:ROWS] + yrecv_t[...].astype(f32)[:ROWS]
    tg_ref[...] = norm_backward(text_values, text_inverse, text_total).astype(bf16)
    store(0, tg_ref, tg_out).start()

    for index in range(PIECES):
        @pl.when(d != index)
        def _(index=index):
            numbered(again, 0, index, wa.at[index], wa.at[index], sibling).wait_recv()
    for index in range(PIECES):
        first = (index // 3) * PIECE_ROWS
        count = min(PIECE_ROWS, ROWS - first)
        columns = pl.ds((index % 3) * PIECE_COLS, PIECE_COLS)
        pg_ref[pl.ds(first, count), columns] = wa[index][:count]

    store(2, pg_ref, pg_out).start()

    assert len(keys) <= SEMS - 32
    for copy in sent.values():
        (copy if isinstance(copy, Block) else copy()).wait_send()

    @pl.when(not_owner)
    def _():
        for part in range(2):
            to_owner(part).wait_send()
        for name in gathered:
            same("share", name, x, sibling).wait_send()

    @pl.when(owner)
    def _():
        for tile in range(tiles):
            gp_copy("yg", tile, x, other_ylo).wait_send()
        for name in gathered:
            same("across", name, x, other_ylo).wait_send()

    for index in range(PIECES):
        @pl.when(d != index)
        def _(index=index):
            scatter(index).wait_send()

    @pl.when(d < PIECES)
    def _():
        for index in range(16):
            @pl.when(d != index)
            def _(index=index):
                gather(index).wait_send()

    for at, (held, target) in enumerate(((tg_ref, tg_out), (fg_ref, fg_out), (pg_ref, pg_out))):
        store(at, held, target).wait()


def local(image_features, proj_weight, text_embed, text_match, logit_scale, logit_bias):
    anywhere = pl.BlockSpec(memory_space=pl.ANY)
    smem = pl.BlockSpec(memory_space=pltpu.SMEM)
    block = (BLOCK, EMBED)
    square = (GROUP, EMBED)
    tail = BLOCK - HEAD
    scratch = [
        pltpu.VMEM((ROWS, GROUP), bf16),
        pltpu.VMEM((ROWS, EMBED), bf16),
        pltpu.VMEM((ROWS, EMBED), bf16),
        pltpu.VMEM((1, ROWS), jnp.int32),
        pltpu.VMEM((ROWS, EMBED), bf16),
        pltpu.VMEM((ROWS, GROUP), bf16),
        pltpu.VMEM((ROWS, EMBED), bf16),
        pltpu.VMEM((2, PAD, EMBED), bf16),
        pltpu.VMEM((2, PAD, EMBED), bf16),
        pltpu.VMEM(square, bf16),
        pltpu.VMEM((GROUP // TILE, GROUP, TILE), bf16),
        pltpu.VMEM((PAD, EMBED), bf16),
        pltpu.VMEM((PAD, EMBED), bf16),
        pltpu.VMEM((8, 128), jnp.int32),
        pltpu.VMEM((8, 128), jnp.int32),
        pltpu.VMEM(square, bf16),
        pltpu.VMEM((8, 8, 128), jnp.int32),
        pltpu.VMEM((2, GROUP, 128), jnp.int32),
        pltpu.VMEM(square, f32),
        pltpu.VMEM(square, bf16),
        pltpu.VMEM((2, CHUNK, TILE), f32),
        pltpu.VMEM(square, bf16),
        pltpu.VMEM(square, f32),
        pltpu.VMEM(square, f32),
        pltpu.VMEM((8,) + block, bf16),
        pltpu.VMEM((HEAD, EMBED), bf16),
        pltpu.VMEM((tail, EMBED), bf16),
        pltpu.VMEM((3,) + block, bf16),
        pltpu.VMEM((3,) + block, bf16),
        pltpu.VMEM((PAD, EMBED), bf16),
        pltpu.VMEM((PAD, EMBED), bf16),
        pltpu.VMEM((4,) + block, bf16),
        pltpu.VMEM((4,) + block, bf16),
        pltpu.VMEM((3,) + block, bf16),
        pltpu.VMEM((HEAD, EMBED), bf16),
        pltpu.VMEM((tail, EMBED), bf16),
        pltpu.VMEM(block, bf16),
        pltpu.VMEM(block, bf16),
        pltpu.VMEM(block, bf16),
        pltpu.VMEM(block, bf16),
        pltpu.VMEM(block, f32),
        pltpu.VMEM((GROUP // TILE, GROUP, TILE), bf16),
        pltpu.VMEM((PAD, EMBED), bf16),
        pltpu.VMEM((16, PIECE_ROWS, PIECE_COLS), bf16),
        pltpu.VMEM((16, PIECE_ROWS, PIECE_COLS), bf16),
        pltpu.SemaphoreType.DMA((SEMS,)),
        pltpu.SemaphoreType.DMA((SEMS,)),
        pltpu.SemaphoreType.DMA((7,)),
    ]
    rows = text_embed.shape[0]
    grads = pl.pallas_call(
        kernel,
        out_shape=jax.ShapeDtypeStruct((3, rows, EMBED), bf16),
        in_specs=[smem, smem, anywhere, anywhere, anywhere, anywhere],
        out_specs=anywhere,
        scratch_shapes=scratch,
        compiler_params=pltpu.CompilerParams(
            collective_id=0, has_side_effects=True, vmem_limit_bytes=60 * 1024 * 1024
        ),
        cost_estimate=pl.CostEstimate(flops=13_000_000_000, bytes_accessed=1_500_000, transcendentals=2_700_000),
    )(logit_scale, logit_bias, image_features, proj_weight, text_embed, text_match.reshape(1, rows))
    return grads[0], grads[1], grads[2].astype(f32)


def solution(mesh):
    return jax.shard_map(
        local,
        mesh=mesh,
        in_specs=(P("mp", "dp"), P("mp", None), P(("dp", "mp"), None), P(("dp", "mp")), P(), P()),
        out_specs=(P(("dp", "mp"), None), P("mp", "dp"), P("mp", None)),
        check_vma=False,
    )
```

```python
import functools

import jax
import jax.numpy as jnp
from jax import lax
from jax.experimental import pallas as pl
from jax.experimental.pallas import tpu as pltpu
from jax.sharding import PartitionSpec as P

MESH = pl.DeviceIdType.MESH
norm_floor = 1e-06
f32, bf16 = jnp.float32, jnp.bfloat16

ZS, XS = 8, 4
ROWS = 72
PAD = 80
BLOCK = 144
HEAD = 80
TEXT_PARTS = ((0, 64), (64, 48), (112, 32))
FIRST = 48
GROUP = 1152
EMBED = 1152
CHUNK = 288
TILE = 384
PIECE = 96
TEXT_ORDER = (0, -1, 1, -2, 2, -3, 3, 4)
TEXT_POS = {step: at for at, step in enumerate(TEXT_ORDER)}
PIECES, PIECE_ROWS, PIECE_COLS = 15, 16, 384
SEMS = 192


def inverse_norm(values):
    return lax.rsqrt(jnp.sum(values * values, axis=1, keepdims=True) + norm_floor)


def norm_backward(values, inverse, upstream):
    along = jnp.sum(values * upstream, axis=1, keepdims=True)
    return inverse * upstream - inverse * inverse * inverse * along * values


def kernel(
    scale_ref, bias_ref, f_in, w_in, t_in, m_in,
    all_out,
    f_ref, w_ref, t_ref, m_ref, tg_ref, fg_ref, pg_ref,
    xsend, xrecv, wf, ff, tsend, trecv, msend, mrecv, tn, mt, mcol, proj, unit, logits, coef, dt, du,
    tout, tra, tlb, tr, tl, ysend_t, yrecv_t,
    csend, crecv, xout, xra, xlb, xr, xl, yout, yin, mine_sum, gp,
    ws, wr, wa,
    send_sem, recv_sem, local_sem,
):
    tg_out, fg_out, pg_out = (all_out.at[at] for at in range(3))
    loads = [
        pltpu.make_async_copy(source, held, local_sem.at[at])
        for at, (source, held) in enumerate(((t_in, t_ref), (w_in, w_ref), (f_in, f_ref), (m_in, m_ref)))
    ]
    for load in loads:
        load.start()

    def store(at, held, target):
        return pltpu.make_async_copy(held, target, local_sem.at[4 + at])

    d, m = lax.axis_index("dp"), lax.axis_index("mp")
    z, yhi = d // 2, d % 2
    x, ylo, core = m // 4, (m // 2) % 2, m % 2

    def at_z(step):
        return {"dp": lax.rem(z + step + ZS, ZS) * 2 + yhi, "mp": m}

    beside_x = {
        way: {"dp": d, "mp": lax.rem(x + way + XS, XS) * 4 + ylo * 2 + core} for way in (1, -1)
    }

    def at_x(way):
        return beside_x[way]

    other_yhi = {"dp": z * 2 + (1 - yhi), "mp": m}
    other_ylo = {"dp": d, "mp": x * 4 + (1 - ylo) * 2 + core}
    sibling = {"dp": d, "mp": x * 4 + ylo * 2 + (1 - core)}

    def dp_at(index):
        return {"dp": index, "mp": m}

    barrier = pltpu.get_barrier_semaphore()
    partners = [sibling, other_ylo, other_yhi, at_x(1), at_x(-1), at_z(1), at_z(-1)]
    for partner in partners:
        pl.semaphore_signal(barrier, inc=1, device_id=partner, device_id_type=MESH)

    keys = {}

    def key(name):
        return keys.setdefault(name, len(keys))

    def describe(name, src, dst, target):
        k = key(name)
        return pltpu.make_async_remote_copy(
            src_ref=src, dst_ref=dst, send_sem=send_sem.at[k], recv_sem=recv_sem.at[k],
            device_id=target, device_id_type=MESH,
        )

    sent = {}

    def start(name, src, dst, target):
        copy = describe(name, src, dst, target)
        copy.start()
        sent[name] = lambda: copy

    def arrived(name, dst, target=sibling):
        describe(name, dst, dst, target).wait_recv()

    for load in loads:
        load.wait()
    f_mine, w_mine = f_ref[...].astype(f32), w_ref[...].astype(f32)
    is_first = core == 0
    owner = ylo == core
    not_owner = jnp.logical_not(owner)
    left_x, right_x, far_x = lax.rem(x + 3, XS), lax.rem(x + 1, XS), lax.rem(x + 2, XS)
    parts = ((0, HEAD), (HEAD, BLOCK - HEAD))
    pad_rows = jnp.zeros((PAD - ROWS, EMBED), f32)
    xsend[0] = jnp.concatenate([w_mine, pad_rows]).astype(bf16)
    xsend[1] = jnp.concatenate([f_mine, pad_rows]).astype(bf16)
    text_values = t_ref[...].astype(f32)
    text_inverse = inverse_norm(text_values)
    text_mine = text_values * text_inverse
    tsend[...] = jnp.concatenate([text_mine, pad_rows]).astype(bf16)
    msend[...] = jnp.zeros_like(msend)
    msend[0:1, 0:ROWS] = m_ref[...]
    pl.semaphore_wait(barrier, len(partners))

    start("x0", xsend, xrecv, sibling)

    def text_rows(step, part):
        first, count = TEXT_PARTS[part]
        return pl.ds(TEXT_POS[step] * BLOCK + first, count)

    def text_forward(step, part, way, new_step):
        start(("t", new_step, part), tn.at[text_rows(step, part)], tn.at[text_rows(new_step, part)], at_z(way))
        if part == 2:
            start(("m", new_step), mt.at[TEXT_POS[step]], mt.at[TEXT_POS[new_step]], at_z(way))

    def text_arrived(step, part):
        arrived(("t", step, part), tn.at[text_rows(step, part)])
        if part == 2:
            arrived(("m", step), mt.at[TEXT_POS[step]])

    near = TEXT_PARTS[0][1]
    tn[pl.ds(0, near), :] = text_mine[:near].astype(bf16)
    text_forward(0, 0, 1, -1)
    text_forward(0, 0, -1, 1)
    start("t0", tsend.at[pl.ds(0, FIRST)], trecv.at[pl.ds(0, FIRST)], other_yhi)
    start("t1", tsend.at[pl.ds(FIRST, PAD - FIRST)], trecv.at[pl.ds(FIRST, PAD - FIRST)], other_yhi)
    start("m0", msend, mrecv, other_yhi)

    def block_rows(from_x, which, part=None):
        first, count = (0, BLOCK) if part is None else parts[part]
        return pl.ds(pl.multiple_of(from_x * CHUNK + which * BLOCK + first, 16), count)

    def block_of(name, from_x, which, part=None):
        rows = block_rows(from_x, which, part)
        return wf.at[rows] if name == "w" else ff.at[:, rows]

    def by_role(of_owner, of_other):
        pl.when(owner)(of_owner)
        pl.when(not_owner)(of_other)

    def by_core(run):
        for index in range(2):
            pl.when(core == index)(functools.partial(run, index))

    class Block:
        def __init__(self, name, what, from_x, which, target, halves=False):
            self.name, self.what, self.from_x, self.which = name, what, from_x, which
            self.target, self.halves = target, halves

        def describe(self, part=None, target=None):
            block = block_of(self.what, self.from_x, self.which, part)
            return describe(self.name, block, block, self.target if target is None else target)

        def run(self, method, mine=True):
            if self.halves:
                by_core(lambda index: getattr(self.describe(index if mine else 1 - index), method)())
            else:
                getattr(self.describe(), method)()

        def start(self):
            self.run("start")
            sent[self.name] = self

        def arrive(self, mine=True):
            self.run("wait_recv", mine)

        def wait_send(self):
            self.run("wait_send")

    way_x = lax.rem(x + 1 + 2 * core, XS)
    ahead = {"dp": d, "mp": way_x * 4 + ylo * 2 + core}
    behind_x = lax.rem(x + 3 + 2 * core, XS)
    other_behind_x = lax.rem(x + 1 + 2 * core, XS)
    other_y = 1 - ylo

    def w_pair(name, from_mine, from_theirs, which, target, halves):
        return Block(name, "w", from_mine, which, target, halves), Block(name, "w", from_theirs[0], from_theirs[1], target, halves)

    w_own, w_behind = w_pair("w1", x, (behind_x, ylo), ylo, ahead, False)
    w_on, w_far = w_pair("w2", behind_x, (far_x, ylo), ylo, ahead, True)
    y_own, y_own_in = w_pair("y0", x, (x, other_y), ylo, other_ylo, True)
    y_behind, y_behind_in = w_pair("y1", behind_x, (behind_x, other_y), ylo, other_ylo, False)
    y_far, y_far_in = w_pair("y2", far_x, (far_x, other_y), ylo, other_ylo, True)

    def w_share(name, from_x, which, halves):
        theirs = other_behind_x if not halves else from_x
        return w_pair(name, from_x, (theirs, which), which, sibling, halves)

    shares = {
        "s1": w_share("s1", behind_x, ylo, False),
        "s2": w_share("s2", far_x, ylo, True),
        "s3": w_share("s3", x, other_y, True),
        "s4": w_share("s4", behind_x, other_y, False),
        "s5": w_share("s5", far_x, other_y, True),
    }

    def same(kind, name, from_x, target, part=None):
        block = block_of(name, from_x, core, part)
        return describe((kind, name, part), block, block, target)

    def move(kind, name, from_x, target, part=None):
        same(kind, name, from_x, target, part).start()
        sent[(kind, name, part)] = functools.partial(same, kind, name, from_x, target, part)

    def came(kind, name, from_x, part=None):
        same(kind, name, from_x, sibling, part).wait_recv()

    tiles = GROUP // TILE
    gathered = ("f",)

    def spread(name):
        move("right", name, x, at_x(1))
        move("left", name, x, at_x(-1))

    def spread_other(name):
        same("across", name, x, other_ylo).wait_recv()
        spread(name)
        same("share", name, x, sibling).start()

    def far(name):
        came("right", name, left_x)
        move("far", name, left_x, at_x(1), 0)
        move("share_left", name, left_x, sibling)
        came("left", name, right_x)
        move("far", name, right_x, at_x(-1), 1)
        move("share_right", name, right_x, sibling)

    def finish(name):
        for part in range(2):
            came("far", name, far_x, part)
            move("share_far", name, far_x, sibling, part)

    def complete(name):
        for kind, from_x, part in (
            ("share_left", left_x, None), ("share_right", right_x, None),
            ("share_far", far_x, 0), ("share_far", far_x, 1),
        ):
            block = block_of(name, from_x, 1 - core, part)
            describe((kind, name, part), block, block, sibling).wait_recv()

        @pl.when(owner)
        def _():
            block = block_of(name, x, 1 - core)
            describe(("share", name, None), block, block, sibling).wait_recv()

    arrived("x0", xrecv)
    for index, own in enumerate((w_mine, f_mine)):
        theirs = xrecv[index].astype(f32)[:ROWS]
        packed = jnp.concatenate(
            [jnp.where(is_first, own, theirs), jnp.where(is_first, theirs, own)]
        ).astype(bf16)
        rows = block_rows(x, ylo)
        if index == 0:
            wf[rows, :] = packed
        else:
            for tile in range(tiles):
                ff[tile, rows, :] = packed[:, tile * TILE:(tile + 1) * TILE]

    w_own.start()

    @pl.when(owner)
    def _():
        same("across", "f", x, other_ylo).start()
        spread("f")

    y_own.start()

    def text_pass(step, part):
        for way in (1, -1):
            text_arrived(-way * step, part)
            text_forward(-way * step, part, way, -way * (step + 1))

    text_pass(1, 0)
    arrived("t0", trecv.at[pl.ds(0, FIRST)])
    taken = TEXT_PARTS[1][1] - (ROWS - near)
    tn[text_rows(0, 1), :] = jnp.concatenate(
        [tsend[...].astype(f32)[near:ROWS], trecv[pl.ds(0, FIRST), :].astype(f32)[:taken]]
    ).astype(bf16)
    text_forward(0, 1, 1, -1)
    text_forward(0, 1, -1, 1)
    arrived("t1", trecv.at[pl.ds(FIRST, PAD - FIRST)])
    arrived("m0", mrecv)
    tn[text_rows(0, 2), :] = trecv[...].astype(f32)[taken:ROWS].astype(bf16)
    mt[0, 0:1, :] = msend[0:1, :]
    mt[0, 1:2, :] = mrecv[0:1, :]
    mt[0, 2:8, :] = jnp.zeros((6, 128), jnp.int32)
    text_forward(0, 2, 1, -1)
    text_forward(0, 2, -1, 1)

    row_number = lax.broadcasted_iota(jnp.int32, (ROWS, 128), 0)

    def columns_of(step):
        place = TEXT_POS[step]
        from_z = lax.rem(z + step + ZS, ZS)
        for which, high in enumerate((yhi, 1 - yhi)):
            row = mt[place, which:which + 1, :]
            column = jnp.transpose(jnp.broadcast_to(row, (128, 128)))[:ROWS]
            rows = pl.ds(place * BLOCK + which * ROWS, ROWS)
            mcol[0, rows, :] = column
            mcol[1, rows, :] = ((from_z * 2 + high) * 16 + m) * ROWS + row_number

    w_behind.arrive()
    w_on.start()
    y_behind.start()
    shares["s1"][0].start()
    by_role(functools.partial(far, "f"), functools.partial(spread_other, "f"))
    columns_of(0)
    text_pass(2, 0)
    y_own_in.arrive()
    shares["s3"][0].start()
    text_pass(1, 1)
    text_pass(1, 2)
    w_far.arrive()
    y_far.start()
    shares["s2"][0].start()
    text_arrived(-3, 0)
    text_forward(-3, 0, 1, 4)
    by_role(functools.partial(finish, "f"), functools.partial(far, "f"))
    columns_of(-1)
    columns_of(1)
    text_pass(2, 1)
    y_behind_in.arrive()
    shares["s4"][0].start()
    text_pass(2, 2)
    text_arrived(3, 0)
    columns_of(-2)
    columns_of(2)
    pl.when(not_owner)(functools.partial(finish, "f"))
    y_far_in.arrive()
    shares["s5"][0].start()
    text_arrived(3, 1)
    text_forward(3, 1, -1, 4)
    complete("f")
    for name in ("s1", "s2", "s3", "s4", "s5"):
        shares[name][1].arrive(mine=False)

    def project(tile):
        values = lax.dot_general(ff[tile], wf[...], (((0,), (0,)), ((), ())), preferred_element_type=f32)
        normal = (values * inverse_norm(values)).astype(bf16)
        for part in range(TILE // PIECE):
            piece = tile * (TILE // PIECE) + part
            away = lax.rem(piece // (CHUNK // PIECE) - x + XS, XS)
            place = jnp.where(away == 2, 0, jnp.where(away == 1, 1, jnp.where(away == 3, 2, 3)))
            row = pl.multiple_of(place * CHUNK + (piece % (CHUNK // PIECE)) * PIECE, PIECE)
            proj[pl.ds(row, PIECE), :] = values[part * PIECE:(part + 1) * PIECE]
            unit[pl.ds(row, PIECE), :] = normal[part * PIECE:(part + 1) * PIECE]

    image_x = (far_x, right_x, left_x, x)
    lane = lax.broadcasted_iota(jnp.int32, (1, GROUP), 1)
    image_number = jnp.zeros_like(lane)
    for place, from_x in enumerate(image_x):
        first = d * GROUP + (from_x - place) * CHUNK
        image_number = jnp.where(lane // CHUNK == place, first + lane, image_number)

    log2e = 1.4426950408889634
    scaling = scale_ref[0]
    slope, shift = scaling * log2e, bias_ref[0] * log2e

    def products_of(buffer, chunk, tile):
        logits[buffer] = lax.dot_general(
            tn[pl.ds(chunk * CHUNK, CHUNK), :], unit[pl.ds(pl.multiple_of(tile * TILE, TILE), TILE), :],
            (((1,), (1,)), ((), ())), preferred_element_type=f32,
        )

    def signs_of(buffer, chunk, tile):
        images = pl.ds(pl.multiple_of(tile * TILE, TILE), TILE)
        image_index = image_number[:, tile * TILE:(tile + 1) * TILE]
        count = 16
        for at in range(0, CHUNK, count):
            here = pl.ds(chunk * CHUNK + at, count)
            match = jnp.concatenate([mcol[0, here, :]] * (TILE // 128), axis=1)
            index = jnp.concatenate([mcol[1, here, :]] * (TILE // 128), axis=1)
            positive = (index == image_index) | (match == image_index)
            power = slope * logits[buffer, pl.ds(at, count), :] + shift
            grown = 1.0 + jnp.exp2(jnp.where(positive, power, -power))
            coef[here, images] = (
                jnp.where(positive, -scaling, scaling) * pl.reciprocal(grown, approx=True)
            ).astype(bf16)

    def coefficients_of(*units):
        for at, unit_at in enumerate(units):
            if at == 0:
                products_of(0, *unit_at)
            if at + 1 < len(units):
                products_of((at + 1) % 2, *units[at + 1])
            signs_of(at % 2, *unit_at)

    project(0)
    text_arrived(3, 2)
    text_forward(3, 2, -1, 4)
    project(1)
    project(2)
    coefficients_of((0, 0), (0, 1), (0, 2), (1, 0), (1, 1), (1, 2))
    text_arrived(-3, 1)
    text_arrived(-3, 2)
    columns_of(-3)
    coefficients_of((2, 0), (2, 1), (2, 2))
    text_arrived(4, 0)
    text_arrived(4, 1)
    text_arrived(4, 2)
    columns_of(3)
    columns_of(4)

    def image_tile(tile):
        columns = pl.ds(pl.multiple_of(tile * TILE, TILE), TILE)
        du[columns, :] = lax.dot_general(
            coef[:, columns], tn[...], (((0,), (0,)), ((), ())), preferred_element_type=f32
        )

    def text_tile(chunk):
        rows = pl.ds(chunk * CHUNK, CHUNK)
        dt[rows, :] = jnp.dot(coef[rows, :], unit[...], preferred_element_type=f32)

    def image_block(place, which, first=0, count=BLOCK):
        return pl.ds(pl.multiple_of(place * CHUNK + which * BLOCK + first, 16), count)

    def to_sibling(place):
        csend[place] = du[image_block(place, 1 - core), :].astype(bf16)
        start(("c", place), csend.at[place], crecv.at[place], sibling)

    def with_sibling(place, part):
        first, count = parts[part]
        return du[image_block(place, core, first, count), :] + crecv[place, pl.ds(first, count), :].astype(f32)

    def image_send(place, part, way, buffer, extra=None):
        first, count = parts[part]
        values = with_sibling(place, part)
        if extra is not None:
            values = values + extra
        xout[place, pl.ds(first, count), :] = values.astype(bf16)
        there = buffer.at[pl.ds(first, count)] if buffer.shape[0] == BLOCK else buffer
        start(("x", place, part, way), xout.at[place, pl.ds(first, count)], there, at_x(way))

    def image_arrived(place, part, way, buffer):
        first, count = parts[part]
        there = buffer.at[pl.ds(first, count)] if buffer.shape[0] == BLOCK else buffer
        arrived(("x", place, part, way), there)
        return there[...].astype(f32)

    def text_partial(step, part):
        first, count = parts[part]
        return dt[pl.ds(TEXT_POS[step] * BLOCK + first, count), :]

    def text_buffer(way, away, part):
        first, count = parts[part]
        if away == 4:
            return tra if way == 1 else tlb
        return (tr if way == 1 else tl).at[3 - away, pl.ds(first, count)]

    def text_came(way, away, part):
        there = text_buffer(way, away, part)
        arrived(("ts", way, away, part), there)
        return there[...].astype(f32)

    def text_send(way, away, part):
        first, count = parts[part]
        step = 4 if away == 4 else way * away
        values = text_partial(step, part)
        if away == 2 or away == 1 or (away == 3 and part == (0 if way == 1 else 1)):
            values = values + text_came(way, away + 1, part)
        place = TEXT_POS[step]
        tout[place, pl.ds(first, count), :] = values.astype(bf16)
        start(
            ("ts", way, away, part), tout.at[place, pl.ds(first, count)], text_buffer(way, away, part), at_z(way)
        )

    products_of(0, 3, 0)
    products_of(1, 3, 1)
    signs_of(0, 3, 0)
    products_of(0, 3, 2)
    image_tile(0)
    to_sibling(0)
    signs_of(1, 3, 1)
    image_tile(1)
    to_sibling(1)
    arrived(("c", 0), crecv.at[0])
    image_send(0, 0, 1, xra)
    image_send(0, 1, -1, xlb)
    signs_of(0, 3, 2)
    image_tile(2)
    to_sibling(2)
    to_sibling(3)
    arrived(("c", 1), crecv.at[1])
    image_send(1, 1, 1, xr)
    text_tile(3)
    text_send(1, 4, 0)
    text_send(-1, 4, 1)
    arrived(("c", 2), crecv.at[2])
    image_send(2, 0, -1, xl)
    text_send(1, 3, 1)
    text_tile(2)
    text_send(-1, 3, 0)
    image_send(1, 0, 1, xr, image_arrived(0, 0, 1, xra))
    image_send(2, 1, -1, xl, image_arrived(0, 1, -1, xlb))
    text_tile(1)
    text_tile(0)
    text_send(1, 3, 0)
    text_send(-1, 3, 1)
    arrived(("c", 3), crecv.at[3])

    text_send(1, 2, 1)
    text_send(-1, 2, 0)

    def to_owner(part):
        rows = pl.ds(*parts[part])
        return describe(("yo", part), yout.at[rows], yin.at[rows], other_ylo)

    for part in range(2):
        rows = pl.ds(*parts[part])
        mine_sum[rows, :] = (
            with_sibling(3, part) + image_arrived(1, part, 1, xr) + image_arrived(2, part, -1, xl)
        )

        @pl.when(not_owner)
        def _(rows=rows, part=part):
            yout[rows, :] = mine_sum[rows, :].astype(bf16)
            to_owner(part).start()

    text_send(1, 2, 0)
    text_send(-1, 2, 1)

    def gp_copy(kind, tile, from_x, target, part=None):
        block = gp.at[tile, block_rows(from_x, core, part)]
        return describe((kind, tile, part), block, block, target)

    def gp_move(kind, tile, from_x, target, part=None):
        gp_copy(kind, tile, from_x, target, part).start()
        sent[(kind, tile, part)] = functools.partial(gp_copy, kind, tile, from_x, target, part)

    def gp_came(kind, tile, from_x, part=None):
        gp_copy(kind, tile, from_x, sibling, part).wait_recv()

    def gp_spread(tile):
        gp_move("gr", tile, x, at_x(1))
        gp_move("gl", tile, x, at_x(-1))
        gp_move("gs", tile, x, sibling)

    @pl.when(owner)
    def _():
        for part in range(2):
            first, count = parts[part]
            to_owner(part).wait_recv()
            total = mine_sum[pl.ds(first, count), :] + yin[pl.ds(first, count), :].astype(f32)
            projected = proj[image_block(3, core, first, count), :]
            result = norm_backward(projected, inverse_norm(projected), total).astype(bf16)
            for tile in range(tiles):
                gp[tile, block_rows(x, core, part), :] = result[:, tile * TILE:(tile + 1) * TILE]
        for tile in range(tiles):
            gp_copy("yg", tile, x, other_ylo).start()
            gp_spread(tile)

    @pl.when(not_owner)
    def _():
        for tile in range(tiles):
            gp_copy("yg", tile, x, other_ylo).wait_recv()
            gp_spread(tile)

    def gp_far(tile):
        gp_came("gr", tile, left_x)
        gp_move("gf", tile, left_x, at_x(1), 0)
        gp_move("gs_left", tile, left_x, sibling)
        gp_came("gl", tile, right_x)
        gp_move("gf", tile, right_x, at_x(-1), 1)
        gp_move("gs_right", tile, right_x, sibling)

    def gp_finish(tile):
        for part in range(2):
            gp_came("gf", tile, far_x, part)
            gp_move("gs_far", tile, far_x, sibling, part)

    def gp_complete(tile):
        for kind, from_x, part in (
            ("gs", x, None), ("gs_left", left_x, None), ("gs_right", right_x, None),
            ("gs_far", far_x, 0), ("gs_far", far_x, 1),
        ):
            block = gp.at[tile, block_rows(from_x, 1 - core, part)]
            describe((kind, tile, part), block, block, sibling).wait_recv()

    text_send(1, 1, 1)
    text_send(-1, 1, 0)
    gp_far(0)
    gp_far(1)
    gp_finish(0)
    gp_far(2)
    text_send(1, 1, 0)
    text_send(-1, 1, 1)

    def piece_of(index):
        rows = pl.ds(pl.multiple_of((index // 3) * PIECE_ROWS, PIECE_ROWS), PIECE_ROWS)
        columns = pl.ds(pl.multiple_of((index % 3) * PIECE_COLS, PIECE_COLS), PIECE_COLS)
        return rows, columns

    def numbered(base, to, source, src, dst, target):
        return pltpu.make_async_remote_copy(
            src_ref=src, dst_ref=dst, send_sem=send_sem.at[base + to], recv_sem=recv_sem.at[base + source],
            device_id=target, device_id_type=MESH,
        )

    base = SEMS - 32
    again = SEMS - 16

    def scatter(index):
        rows, columns = piece_of(index)
        return numbered(base, index, d, ws.at[rows, columns], wr.at[d], dp_at(index))

    def gather(index):
        return numbered(again, index, d, wa.at[d], wa.at[d], dp_at(index))

    def weight_tile(tile):
        gp_complete(tile)
        part = jnp.dot(f_ref[...], gp[tile], preferred_element_type=f32)
        ws[:, tile * TILE:(tile + 1) * TILE] = jnp.concatenate([part, pad_rows[:, :TILE]]).astype(bf16)
        for index in range(tile, PIECES, tiles):
            @pl.when(d != index)
            def _(index=index):
                scatter(index).start()

    def reduce_piece():
        rows, columns = piece_of(d)
        wr[d] = ws[rows, columns]
        for source in range(16):
            @pl.when(d != source)
            def _(source=source):
                numbered(base, 0, source, wr.at[source], wr.at[source], sibling).wait_recv()
        total = wr[0].astype(f32)
        for source in range(1, 16):
            total = total + wr[source].astype(f32)
        wa[d] = total.astype(bf16)
        for step in (8, 7, 9, 6, 10, 5, 11, 4, 12, 3, 13, 2, 14, 1, 15):
            gather(lax.rem(d + step, 16)).start()

    weight_tile(0)
    gp_finish(1)
    gp_finish(2)
    weight_tile(1)

    weight_tile(2)
    pl.when((d < PIECES) & (d % 3 == 0))(reduce_piece)
    feature = lax.dot_general(
        w_ref[:, :TILE], gp[0], (((1,), (1,)), ((), ())), preferred_element_type=f32
    )
    for tile in range(1, tiles):
        feature = feature + lax.dot_general(
            w_ref[:, tile * TILE:(tile + 1) * TILE], gp[tile], (((1,), (1,)), ((), ())), preferred_element_type=f32
        )
    fg_ref[...] = feature.astype(bf16)
    store(1, fg_ref, fg_out).start()

    total = jnp.concatenate(
        [text_partial(0, part) + text_came(1, 1, part) + text_came(-1, 1, part) for part in range(2)]
    )
    ysend_t[...] = jnp.concatenate([total[ROWS:], pad_rows]).astype(bf16)
    start("ty", ysend_t, yrecv_t, other_yhi)

    pl.when((d < PIECES) & (d % 3 != 0))(reduce_piece)

    arrived("ty", yrecv_t)
    text_total = total[:ROWS] + yrecv_t[...].astype(f32)[:ROWS]
    tg_ref[...] = norm_backward(text_values, text_inverse, text_total).astype(bf16)
    store(0, tg_ref, tg_out).start()

    for index in range(PIECES):
        @pl.when(d != index)
        def _(index=index):
            numbered(again, 0, index, wa.at[index], wa.at[index], sibling).wait_recv()
    for index in range(PIECES):
        first = (index // 3) * PIECE_ROWS
        count = min(PIECE_ROWS, ROWS - first)
        columns = pl.ds((index % 3) * PIECE_COLS, PIECE_COLS)
        pg_ref[pl.ds(first, count), columns] = wa[index][:count]

    store(2, pg_ref, pg_out).start()

    assert len(keys) <= SEMS - 32
    for copy in sent.values():
        (copy if isinstance(copy, Block) else copy()).wait_send()

    @pl.when(not_owner)
    def _():
        for part in range(2):
            to_owner(part).wait_send()
        for name in gathered:
            same("share", name, x, sibling).wait_send()

    @pl.when(owner)
    def _():
        for tile in range(tiles):
            gp_copy("yg", tile, x, other_ylo).wait_send()
        for name in gathered:
            same("across", name, x, other_ylo).wait_send()

    for index in range(PIECES):
        @pl.when(d != index)
        def _(index=index):
            scatter(index).wait_send()

    @pl.when(d < PIECES)
    def _():
        for index in range(16):
            @pl.when(d != index)
            def _(index=index):
                gather(index).wait_send()

    for at, (held, target) in enumerate(((tg_ref, tg_out), (fg_ref, fg_out), (pg_ref, pg_out))):
        store(at, held, target).wait()


def local(image_features, proj_weight, text_embed, text_match, logit_scale, logit_bias):
    anywhere = pl.BlockSpec(memory_space=pl.ANY)
    smem = pl.BlockSpec(memory_space=pltpu.SMEM)
    block = (BLOCK, EMBED)
    square = (GROUP, EMBED)
    tail = BLOCK - HEAD
    scratch = [
        pltpu.VMEM((ROWS, GROUP), bf16),
        pltpu.VMEM((ROWS, EMBED), bf16),
        pltpu.VMEM((ROWS, EMBED), bf16),
        pltpu.VMEM((1, ROWS), jnp.int32),
        pltpu.VMEM((ROWS, EMBED), bf16),
        pltpu.VMEM((ROWS, GROUP), bf16),
        pltpu.VMEM((ROWS, EMBED), bf16),
        pltpu.VMEM((2, PAD, EMBED), bf16),
        pltpu.VMEM((2, PAD, EMBED), bf16),
        pltpu.VMEM(square, bf16),
        pltpu.VMEM((GROUP // TILE, GROUP, TILE), bf16),
        pltpu.VMEM((PAD, EMBED), bf16),
        pltpu.VMEM((PAD, EMBED), bf16),
        pltpu.VMEM((8, 128), jnp.int32),
        pltpu.VMEM((8, 128), jnp.int32),
        pltpu.VMEM(square, bf16),
        pltpu.VMEM((8, 8, 128), jnp.int32),
        pltpu.VMEM((2, GROUP, 128), jnp.int32),
        pltpu.VMEM(square, f32),
        pltpu.VMEM(square, bf16),
        pltpu.VMEM((2, CHUNK, TILE), f32),
        pltpu.VMEM(square, bf16),
        pltpu.VMEM(square, f32),
        pltpu.VMEM(square, f32),
        pltpu.VMEM((8,) + block, bf16),
        pltpu.VMEM((HEAD, EMBED), bf16),
        pltpu.VMEM((tail, EMBED), bf16),
        pltpu.VMEM((3,) + block, bf16),
        pltpu.VMEM((3,) + block, bf16),
        pltpu.VMEM((PAD, EMBED), bf16),
        pltpu.VMEM((PAD, EMBED), bf16),
        pltpu.VMEM((4,) + block, bf16),
        pltpu.VMEM((4,) + block, bf16),
        pltpu.VMEM((3,) + block, bf16),
        pltpu.VMEM((HEAD, EMBED), bf16),
        pltpu.VMEM((tail, EMBED), bf16),
        pltpu.VMEM(block, bf16),
        pltpu.VMEM(block, bf16),
        pltpu.VMEM(block, bf16),
        pltpu.VMEM(block, bf16),
        pltpu.VMEM(block, f32),
        pltpu.VMEM((GROUP // TILE, GROUP, TILE), bf16),
        pltpu.VMEM((PAD, EMBED), bf16),
        pltpu.VMEM((16, PIECE_ROWS, PIECE_COLS), bf16),
        pltpu.VMEM((16, PIECE_ROWS, PIECE_COLS), bf16),
        pltpu.SemaphoreType.DMA((SEMS,)),
        pltpu.SemaphoreType.DMA((SEMS,)),
        pltpu.SemaphoreType.DMA((7,)),
    ]
    rows = text_embed.shape[0]
    grads = pl.pallas_call(
        kernel,
        out_shape=jax.ShapeDtypeStruct((3, rows, EMBED), bf16),
        in_specs=[smem, smem, anywhere, anywhere, anywhere, anywhere],
        out_specs=anywhere,
        scratch_shapes=scratch,
        compiler_params=pltpu.CompilerParams(
            collective_id=0, has_side_effects=True, vmem_limit_bytes=60 * 1024 * 1024
        ),
        cost_estimate=pl.CostEstimate(flops=13_000_000_000, bytes_accessed=1_500_000, transcendentals=2_700_000),
    )(logit_scale, logit_bias, image_features, proj_weight, text_embed, text_match.reshape(1, rows))
    return grads[0], grads[1], grads[2].astype(f32)


def solution(mesh):
    return jax.shard_map(
        local,
        mesh=mesh,
        in_specs=(P("mp", "dp"), P("mp", None), P(("dp", "mp"), None), P(("dp", "mp")), P(), P()),
        out_specs=(P(("dp", "mp"), None), P("mp", "dp"), P("mp", None)),
        check_vma=False,
    )
```
